256 devices in a mesh: row: 16 (over x, y_hi, core), col: 16 (over y_lo, z).
Axes of the slice: x: 4, y: 4 (y_hi: 2, y_lo: 2; y = y_hi * 2 + y_lo), z: 8, core: 2. Of those that a mesh axis runs over, the one named last changes fastest.
Arguments:
- embeddings: bfloat16 [196608, 512], P(('row', 'col')), may hold values from -40 to 40
- positives: int32 [196608], P(('row', 'col')), may hold values from 0 to 767, as said below
Outputs:
- gradient: float32 [196608, 512], P(('row', 'col'))
The draws below stay inside these ranges and needn't reach their ends.
Inputs may be any that keep to these rules, and one draw needn't show every extreme that they name: Within each block of 768 rows the rows are paired off: positives[k] names the position of k's partner in k's block, the partner's partner is k, and no row is its own partner.
All inputs are finite; a program needn't handle non-finite values.
Results may differ from the reference program's by a relative error of at most 0.0051.
Values may be sent and summed in bfloat16 or wider, within the bound.
No kernel may reach another device: no remote copies, remote signals or barrier semaphores. Data moves between devices by JAX's collectives and lax.ppermute only.
A program may use at most 64 MiB of HBM per device.

```python
import jax
import jax.numpy as jnp
from jax import lax

D = 512
ROWS_DEV = 768
BATCH = 196608
N_ROW = 16
N_COL = 16


proto_count = 8


def pair_table(key):
    block_count = BATCH // ROWS_DEV
    subkeys = jax.random.split(key, block_count)

    def one_order(subkey):
        return jax.random.permutation(subkey, ROWS_DEV).astype(jnp.int32)
    orders = jax.vmap(one_order)(subkeys)
    partner = orders.reshape(block_count, ROWS_DEV // 2, 2)[:, :, ::-1].reshape(block_count, ROWS_DEV)

    def place(order, mates):
        return jnp.zeros((ROWS_DEV,), jnp.int32).at[order].set(mates)
    return jax.vmap(place)(orders, partner)


def draw_positives(key, part):
    paired = pair_table(key)
    return paired.reshape(BATCH).astype(jnp.int32)


def draw_embeddings(key, part):
    paired = pair_table(key)
    key = jax.random.fold_in(key, 5)
    block_count = BATCH // ROWS_DEV
    key_mean = jax.random.fold_in(key, 0)
    key_pair = jax.random.fold_in(key, 1)
    key_own = jax.random.fold_in(key, 2)
    key_base = jax.random.fold_in(key, 4)
    key_pick = jax.random.fold_in(key, 5)
    pair_id = jnp.minimum(jnp.arange(ROWS_DEV, dtype=jnp.int32)[None, :], paired)
    picks = jax.random.randint(key_pick, (block_count, ROWS_DEV), 0, 2 * proto_count).astype(jnp.int32)
    picks = jnp.take_along_axis(picks, pair_id, axis=1)
    signs = (1 - 2 * (picks // proto_count)).astype(jnp.float32)[:, :, None]
    base = jax.random.normal(key_base, (proto_count, D), jnp.float32) * 2.0
    means = jax.random.normal(key_mean, (block_count, 1, D), jnp.float32) * 0.3
    shared = jax.random.normal(key_pair, (block_count, ROWS_DEV, D), jnp.float32)
    own = jax.random.normal(key_own, (block_count, ROWS_DEV, D), jnp.float32) * 0.7
    protos = base[picks % proto_count] * signs
    matched = jnp.take_along_axis(shared, pair_id[:, :, None], axis=1)
    values = means + protos + matched + own
    return jnp.clip(values, -40.0, 40.0).reshape(BATCH, D).astype(jnp.bfloat16)


def setup_inputs(seed: int = 0) -> dict:
    key_of = jax.random.split(jax.random.key(seed), 3)
    return {
        "embeddings": draw_embeddings(jax.random.fold_in(key_of[2], 71), 0),
        "positives": draw_positives(jax.random.fold_in(key_of[2], 71), 0),
    }


inverse_temp = 5.0
epsilon = 1e-06

def normalize(values):
    wide = values.astype(jnp.float32)
    return (wide * lax.rsqrt(lax.optimization_barrier(jnp.sum(wide * wide, axis=-1, keepdims=True)) + epsilon)).astype(jnp.bfloat16)

def reference(embeddings, positives):
    count = N_ROW * N_COL
    normed = normalize(embeddings).reshape(count, ROWS_DEV, D)
    paired = positives.reshape(count, ROWS_DEV)
    offsets = [1, N_COL, N_COL + 1, count // 4]
    deltas = jnp.array([0] + [-step for step in offsets] + [step for step in offsets], dtype=jnp.int32)
    diagonal = jnp.arange(ROWS_DEV)[:, None] == jnp.arange(ROWS_DEV)[None, :]
    self_mask = (jnp.arange(deltas.shape[0]) == 0)[:, None, None] & diagonal[None]

    def tiles(block_id):
        neighbours = ((block_id + deltas) % count).astype(jnp.int32)
        partner = normed[neighbours].astype(jnp.float32)
        mine = normed[block_id].astype(jnp.float32)
        scores = jnp.einsum('kd,cjd->ckj', mine, partner, precision=lax.Precision.HIGHEST)
        exps = jnp.where(self_mask, jnp.float32(0.0), jnp.exp(scores * inverse_temp))
        return (exps, neighbours, partner)

    def row_total(block_id):
        exps, neighbours, partner = tiles(block_id)
        return lax.optimization_barrier(jnp.sum(exps, axis=(0, 2)))
    block_ids = jnp.arange(count, dtype=jnp.int32)
    denoms = lax.map(row_total, block_ids)

    def block_gradient(block_id):
        exps, neighbours, partner = tiles(block_id)
        recips = 1.0 / denoms[block_id]
        others = 1.0 / denoms[neighbours]
        weights = (exps * (recips[None, :, None] + others[:, None, :])).astype(jnp.bfloat16)
        total = jnp.einsum('ckj,cjd->kd', weights.astype(jnp.float32), partner, precision=lax.Precision.HIGHEST)
        matched = normed[block_id][paired[block_id]].astype(jnp.float32)
        return inverse_temp * total - 2.0 * inverse_temp * matched
    return lax.map(block_gradient, block_ids).reshape(count * ROWS_DEV, D)
```

```python
import jax
import jax.numpy as jnp
from jax import lax
from jax.sharding import PartitionSpec as P

inverse_temp = 5.0
epsilon = 1e-06
both = ("row", "col")


def routes(rows, cols):
    count = rows * cols
    far_step = cols
    x_step = count // 4

    def wrap(value):
        return value % count

    def core(b):
        return (b // cols) % 2

    def half(b):
        return (b // (2 * cols)) % 2

    def far17(b):
        j = b % cols
        if core(b) == 0:
            if j == 0:
                return wrap(b + (2 * cols if half(b) == 0 else -2 * cols) + cols - 1)
            return wrap(b - 2 * cols - 1) if j == cols // 2 else b - 1
        if j == cols - 1:
            return wrap(b + (2 * cols if half(b) == 0 else -2 * cols) - cols + 1)
        return wrap(b + 2 * cols + 1) if j == cols // 2 - 1 else b + 1

    sources = {
        "above": lambda b: wrap(b + 1),
        "below": lambda b: wrap(b - 1),
        "x_above": lambda b: wrap(b + x_step),
        "x_below": lambda b: wrap(b - x_step),
        "near": lambda b: b + far_step if core(b) == 0 else b - far_step,
        "far": lambda b: wrap(b - far_step if core(b) == 0 else b + far_step),
        "far17": far17,
    }
    return {name: [(source(b), b) for b in range(count)] for name, source in sources.items()}


def exp_tile(mine, theirs):
    scores = lax.dot_general(
        mine, theirs, (((1,), (1,)), ((), ())), preferred_element_type=jnp.float32
    )
    exps = jnp.exp(scores * inverse_temp)
    return exps


def on_device(embeddings, positives):
    row_count = embeddings.shape[0]
    rows, cols = lax.axis_size("row"), lax.axis_size("col")
    route = routes(rows, cols)
    row, col = lax.axis_index("row"), lax.axis_index("col")
    core0 = row % 2 == 0

    def send(block, name):
        return lax.ppermute(block, both, route[name])

    wide = embeddings.astype(jnp.float32)
    normed = (wide * lax.rsqrt(jnp.sum(wide * wide, axis=-1, keepdims=True) + epsilon)).astype(
        jnp.bfloat16
    )
    matched = jnp.take(normed, positives, axis=0).astype(jnp.float32)

    far = send(normed, "far")
    above = send(normed, "above")
    below = send(normed, "below")
    x_above = send(normed, "x_above")
    x_below = send(normed, "x_below")
    near = send(normed, "near")
    last = jnp.where(core0, cols - 1, 0)
    turn = jnp.where(core0, cols // 2 - 1, cols // 2)
    crossing = (row // 2) % 2 == jnp.where(core0, 1, 0)
    passed = jnp.where(
        col == last,
        jnp.where(crossing, jnp.where(core0, x_below, x_above), normed),
        jnp.where(col == turn, near, far),
    )
    far17 = send(passed, "far17")
    near17 = send(jnp.where(core0, below, above), "near")

    diagonal = jnp.arange(row_count)[:, None] == jnp.arange(row_count)[None, :]
    self_tile = jnp.where(diagonal, jnp.float32(0.0), exp_tile(normed, normed))
    denoms = jnp.sum(self_tile, axis=1)
    blocks = [near, above, below, x_above, x_below, far, near17, far17]
    tiles = []
    for block in blocks:
        tile = exp_tile(normed, block)
        denoms = denoms + jnp.sum(tile, axis=1)
        tiles.append(tile.astype(jnp.bfloat16))
    d_above = send(denoms, "above")
    d_below = send(denoms, "below")
    d_x_above = send(denoms, "x_above")
    d_x_below = send(denoms, "x_below")
    trio = jnp.stack([denoms, d_above, d_below])
    near_trio = send(trio, "near")
    far_trio = send(trio, "far")
    d_near, d_far = near_trio[0], far_trio[0]
    d_near17 = jnp.where(core0, near_trio[1], near_trio[2])
    d_far17 = jnp.where(core0, far_trio[2], far_trio[1])
    norms = [d_near, d_above, d_below, d_x_above, d_x_below, d_far, d_near17, d_far17]
    recips = 1.0 / denoms

    def weigh_tile(exps, others):
        return (exps * (recips[:, None] + 1.0 / others[None, :])).astype(jnp.bfloat16)

    gradient = jnp.dot(weigh_tile(self_tile, denoms), normed, preferred_element_type=jnp.float32)
    order = [3, 4, 1, 2, 0, 5, 6, 7]
    for number in order:
        weights = weigh_tile(tiles[number].astype(jnp.float32), norms[number])
        gradient = gradient + jnp.dot(weights, blocks[number], preferred_element_type=jnp.float32)
    return inverse_temp * gradient - 2.0 * inverse_temp * matched


def solution(mesh):
    placed = (P(("row", "col"), None), P(("row", "col")))
    return jax.shard_map(
        on_device, mesh=mesh, in_specs=placed, out_specs=P(("row", "col"), None), check_vma=False
    )
```

```python
import functools

import jax
import jax.numpy as jnp
from jax import lax
from jax.experimental import pallas as pl
from jax.experimental.pallas import tpu as pltpu
from jax.sharding import PartitionSpec as P

inverse_temp = 5.0
epsilon = 1e-06
both = ("row", "col")
lanes = 128
chunk = 256


def routes(rows, cols):
    count = rows * cols
    far_step = cols
    x_step = count // 4
    line = cols // 2

    def wrap(value):
        return value % count

    def core(b):
        return (b // cols) % 2

    def half(b):
        return (b // (2 * cols)) % 2

    def far17(b):
        j = b % cols
        if core(b) == 0:
            if j == 0:
                return wrap(b + (2 * cols if half(b) == 0 else -2 * cols) + cols - 1)
            return wrap(b - 2 * cols - 1) if j == cols // 2 else b - 1
        if j == cols - 1:
            return wrap(b + (2 * cols if half(b) == 0 else -2 * cols) - cols + 1)
        return wrap(b + 2 * cols + 1) if j == cols // 2 - 1 else b + 1

    def ring(step):
        return lambda b: b - b % line + (b + step) % line

    def turn(b):
        return wrap(b + 1) if (b + 1) % line == 0 else wrap(b - 1) if b % line == 0 else b

    def turn_source(b):
        taken = turn(b)
        if taken == b:
            return b
        return taken + line - 1 if taken % line == 0 else taken - line + 1

    sources = {
        "above": lambda b: wrap(b + 1),
        "below": lambda b: wrap(b - 1),
        "ring_above": ring(1),
        "ring_below": ring(-1),
        "turn": turn_source,
        "x_above": lambda b: wrap(b + x_step),
        "x_below": lambda b: wrap(b - x_step),
        "near": lambda b: b + far_step if core(b) == 0 else b - far_step,
        "far": lambda b: wrap(b - far_step if core(b) == 0 else b + far_step),
        "far17": far17,
    }
    return {name: [(source(b), b) for b in range(count)] for name, source in sources.items()}


vmem_limit = 5 * 1024 * 1024
held = pl.BlockSpec(memory_space=pltpu.VMEM)
small = pl.BlockSpec(memory_space=pltpu.VMEM)
anywhere = pl.BlockSpec(memory_space=pl.ANY)


def hold(*arrays):
    return [pltpu.with_memory_space_constraint(array, pltpu.VMEM) for array in arrays]


def call(kernel, name, in_specs, out_specs, out_shape, flops, moved, exps=0, scratch=()):
    return pl.pallas_call(
        kernel,
        in_specs=in_specs,
        out_specs=out_specs,
        out_shape=out_shape,
        scratch_shapes=scratch,
        compiler_params=pltpu.CompilerParams(vmem_limit_bytes=vmem_limit),
        cost_estimate=pl.CostEstimate(flops=flops, bytes_accessed=moved, transcendentals=exps),
        name=name,
    )


def parts(rows):
    return [slice(start, start + chunk) for start in range(0, rows, chunk)]


def normalize_kernel(rows_ref, out_ref, held_ref, sems):
    rows = rows_ref.shape[0]
    copies = []
    for number, part in enumerate(parts(rows)):
        copy = pltpu.make_async_copy(rows_ref.at[part], held_ref.at[part], sems.at[number])
        copy.start()
        copies.append(copy)
    for copy, part in zip(copies, parts(rows)):
        copy.wait()
        wide = held_ref[part, :].astype(jnp.float32)
        scale = lax.rsqrt(jnp.sum(wide * wide, axis=-1, keepdims=True) + epsilon)
        out_ref[part, :] = (wide * scale).astype(jnp.bfloat16)


def normalize(embeddings):
    rows, width = embeddings.shape
    return call(
        normalize_kernel,
        "normalize",
        [anywhere],
        held,
        pltpu.VMEM((rows, width), jnp.bfloat16),
        4 * rows * width,
        4 * rows * width,
        scratch=[
            pltpu.VMEM((rows, width), jnp.bfloat16),
            pltpu.SemaphoreType.DMA((rows // chunk,)),
        ],
    )(pltpu.with_memory_space_constraint(embeddings, pltpu.HBM))


def exps_of(mine, theirs):
    scores = lax.dot_general(
        mine, theirs, (((1,), (1,)), ((), ())), preferred_element_type=jnp.float32
    )
    return jnp.exp(scores * inverse_temp)


def fold(exps):
    total = exps[:, :lanes]
    for start in range(lanes, exps.shape[1], lanes):
        total = total + exps[:, start : start + lanes]
    return total


def self_kernel(mine_ref, pos_ref, exps_ref, sums_ref, matched_ref):
    rows = mine_ref.shape[0]
    pairs = [pos_ref[number : number + 1, :] for number in range(rows // lanes)]
    partners = jnp.concatenate(pairs, axis=1)
    for part in parts(rows):
        k = lax.broadcasted_iota(jnp.int32, (chunk, rows), 0) + part.start
        j = lax.broadcasted_iota(jnp.int32, (chunk, rows), 1)
        exps = jnp.where(k == j, 0.0, exps_of(mine_ref[part, :], mine_ref[...]))
        exps_ref[part, :] = exps.astype(jnp.bfloat16)
        sums_ref[part, :] = fold(exps)
        picks = jnp.where(k == partners, 1.0, 0.0).astype(jnp.bfloat16)
        matched = jnp.dot(picks, mine_ref[...], preferred_element_type=jnp.float32)
        matched_ref[part, :] = matched.astype(jnp.bfloat16)


def self_tile(normed, positives):
    rows, width = normed.shape
    return call(
        self_kernel,
        "self_tile",
        [held, small],
        [held] * 3,
        [
            pltpu.VMEM((rows, rows), jnp.bfloat16),
            pltpu.VMEM((rows, lanes), jnp.float32),
            pltpu.VMEM((rows, width), jnp.bfloat16),
        ],
        4 * rows * rows * width,
        4 * rows * width + 2 * rows * rows,
        rows * rows,
    )(*hold(normed), positives)


def tile_kernel(mine_ref, theirs_ref, before_ref, exps_ref, sums_ref):
    for part in parts(mine_ref.shape[0]):
        exps = exps_of(mine_ref[part, :], theirs_ref[...])
        exps_ref[part, :] = exps.astype(jnp.bfloat16)
        sums_ref[part, :] = before_ref[part, :] + fold(exps)


def pair_tile(normed, block, sums):
    rows, width = normed.shape
    return call(
        tile_kernel,
        "pair_tile",
        [held] * 3,
        [held] * 2,
        [pltpu.VMEM((rows, rows), jnp.bfloat16), pltpu.VMEM((rows, lanes), jnp.float32)],
        2 * rows * rows * width,
        4 * rows * width + 2 * rows * rows,
        rows * rows,
    )(*hold(normed, block, sums))


def last_kernel(mine_ref, theirs_ref, before_ref, exps_ref, sums_ref, denoms_ref):
    for part in parts(mine_ref.shape[0]):
        exps = exps_of(mine_ref[part, :], theirs_ref[...])
        exps_ref[part, :] = exps.astype(jnp.bfloat16)
        sums = before_ref[part, :] + fold(exps)
        sums_ref[part, :] = sums
        denoms_ref[:, part] = jnp.sum(sums.T, axis=0, keepdims=True)


def last_tile(normed, block, sums):
    rows, width = normed.shape
    return call(
        last_kernel,
        "last_tile",
        [held] * 3,
        [held] * 3,
        [
            pltpu.VMEM((rows, rows), jnp.bfloat16),
            pltpu.VMEM((rows, lanes), jnp.float32),
            pltpu.VMEM((1, rows), jnp.float32),
        ],
        2 * rows * rows * width,
        4 * rows * width + 2 * rows * rows,
        rows * rows,
    )(*hold(normed, block, sums))


def far17_kernel(far_ref, near_ref, mine_ref, x_below_ref, x_above_ref, out_ref):
    cols, col = lax.axis_size("col"), lax.axis_index("col")
    row = lax.axis_index("row")
    core0 = row % 2 == 0
    half0 = (row // 2) % 2 == 0
    last = col == jnp.where(core0, cols - 1, 0)
    turn = col == jnp.where(core0, cols // 2 - 1, cols // 2)
    crossing = last & (core0 != half0)
    choices = [
        (crossing & core0, x_below_ref),
        (crossing & ~core0, x_above_ref),
        (last & ~crossing, mine_ref),
        (turn, near_ref),
        (~last & ~turn, far_ref),
    ]
    for chosen, ref in choices:

        @pl.when(chosen)
        def _():
            out_ref[...] = ref[...]


def turn_kernel(above_ref, below_ref, out_ref):
    line = lax.axis_size("col") // 2
    place = lax.axis_index("col") % line

    @pl.when(place == line - 1)
    def _():
        out_ref[...] = above_ref[...]

    @pl.when(place == 0)
    def _():
        out_ref[...] = below_ref[...]


def merge_kernel(shift, ring_ref, turn_ref, out_ref):
    turns = (lax.axis_index("col") + shift) % (lax.axis_size("col") // 2) == 0

    @pl.when(turns)
    def _():
        out_ref[...] = turn_ref[...]

    @pl.when(~turns)
    def _():
        out_ref[...] = ring_ref[...]


def near17_kernel(below_ref, above_ref, out_ref):
    core0 = lax.axis_index("row") % 2 == 0

    @pl.when(core0)
    def _():
        out_ref[...] = below_ref[...]

    @pl.when(~core0)
    def _():
        out_ref[...] = above_ref[...]


def choose(kernel, name, *choices):
    shape = choices[0].shape
    return call(
        kernel,
        name,
        [held] * len(choices),
        held,
        pltpu.VMEM(shape, jnp.bfloat16),
        0,
        4 * shape[0] * shape[1],
    )(*hold(*choices))


def weighted(sums_ref, others, exps_refs, block_refs, part):
    mine = 1.0 / jnp.sum(sums_ref[part, :], axis=1, keepdims=True)
    total = None
    for other, exps_ref, block_ref in zip(others, exps_refs, block_refs):
        weights = exps_ref[part, :].astype(jnp.float32) * (mine + other)
        term = jnp.dot(
            weights.astype(jnp.bfloat16), block_ref[...], preferred_element_type=jnp.float32
        )
        total = term if total is None else total + term
    return total


def first_kernel(count, sums_ref, matched_ref, *refs):
    exps_refs, block_refs = refs[:count], refs[count : 2 * count]
    norm_refs, out_ref = refs[2 * count : 3 * count], refs[3 * count]
    others = [1.0 / norm_ref[...] for norm_ref in norm_refs]
    for part in parts(sums_ref.shape[0]):
        total = weighted(sums_ref, others, exps_refs, block_refs, part)
        out_ref[part, :] = total - 2.0 * matched_ref[part, :].astype(jnp.float32)


def final_kernel(count, sums_ref, first_ref, *refs):
    exps_refs, block_refs = refs[:count], refs[count : 2 * count]
    near_ref, far_ref, out_ref, held_ref, sems = refs[2 * count :]
    core0 = lax.axis_index("row") % 2 == 0
    near17 = jnp.where(core0, near_ref[1:2, :], near_ref[2:3, :])
    far17 = jnp.where(core0, far_ref[2:3, :], far_ref[1:2, :])
    others = [1.0 / norm for norm in (near_ref[0:1, :], far_ref[0:1, :], near17, far17)]
    copies = []
    for number, part in enumerate(parts(sums_ref.shape[0])):
        total = weighted(sums_ref, others, exps_refs, block_refs, part)
        held_ref[part, :] = inverse_temp * (first_ref[part, :] + total)
        copy = pltpu.make_async_copy(held_ref.at[part], out_ref.at[part], sems.at[number])
        copy.start()
        copies.append(copy)
    for copy in copies:
        copy.wait()


def gather_first(sums, matched, exps, blocks, norms):
    count, (rows, width) = len(exps), matched.shape
    return call(
        functools.partial(first_kernel, count),
        "gather_first",
        [held] * (3 * count + 2),
        held,
        pltpu.VMEM((rows, width), jnp.float32),
        2 * count * rows * rows * width,
        count * 2 * rows * (rows + width) + 8 * rows * width,
    )(*hold(sums, matched, *exps, *blocks, *norms))


def gather_final(sums, first, exps, blocks, near_trio, far_trio):
    count, (rows, width) = len(exps), first.shape
    return call(
        functools.partial(final_kernel, count),
        "gather_final",
        [held] * (2 * count + 4),
        anywhere,
        jax.ShapeDtypeStruct((rows, width), jnp.float32),
        2 * count * rows * rows * width,
        count * 2 * rows * (rows + width) + 8 * rows * width,
        scratch=[
            pltpu.VMEM((rows, width), jnp.float32),
            pltpu.SemaphoreType.DMA((rows // chunk,)),
        ],
    )(*hold(sums, first, *exps, *blocks, near_trio, far_trio))


def join_kernel(*refs):
    *parts_refs, out_ref = refs
    for number, ref in enumerate(parts_refs):
        out_ref[number : number + 1, :] = ref[...]


def join(*rows):
    width = rows[0].shape[1]
    return call(
        join_kernel,
        "join",
        [held] * len(rows),
        held,
        pltpu.VMEM((len(rows), width), jnp.float32),
        0,
        8 * len(rows) * width,
    )(*hold(*rows))


def on_device(embeddings, positives):
    rows, cols = lax.axis_size("row"), lax.axis_size("col")
    route = routes(rows, cols)

    def send(block, name):
        return lax.ppermute(block, both, route[name])

    normed = normalize(embeddings)
    near = send(normed, "near")
    ring_above = send(normed, "ring_above")
    ring_below = send(normed, "ring_below")
    far = send(normed, "far")
    x_below = send(normed, "x_below")
    self_exps, sums, matched = self_tile(normed, positives.reshape(-1, lanes))
    later, near, sums = lax.optimization_barrier((normed, near, sums))
    x_above = send(later, "x_above")
    turn = send(choose(turn_kernel, "turn", ring_above, ring_below), "turn")
    passed = choose(far17_kernel, "far17", far, near, normed, x_below, x_above)
    far17 = send(passed, "far17")
    exps, blocks = {}, {}

    def add(sums, **some):
        for name, block in some.items():
            blocks[name] = block
            exps[name], sums = pair_tile(normed, block, sums)
        return sums

    sums = add(sums, near=near, far=far, x_below=x_below, x_above=x_above)
    turn, sums = lax.optimization_barrier((turn, sums))
    above = choose(functools.partial(merge_kernel, 1), "above", ring_above, turn)
    below = choose(functools.partial(merge_kernel, 0), "below", ring_below, turn)
    near17 = send(choose(near17_kernel, "near17", below, above), "near")
    sums = add(sums, above=above, below=below, far17=far17)
    blocks["near17"] = near17
    exps["near17"], sums, denoms = last_tile(normed, near17, sums)

    d_above = send(denoms, "above")
    d_below = send(denoms, "below")
    d_x_above = send(denoms, "x_above")
    d_x_below = send(denoms, "x_below")
    trio = join(denoms, d_above, d_below)
    near_trio = send(trio, "near")
    far_trio = send(trio, "far")

    names = ["above", "below", "x_above", "x_below"]
    first = gather_first(
        sums,
        matched,
        [self_exps] + [exps[name] for name in names],
        [normed] + [blocks[name] for name in names],
        [denoms, d_above, d_below, d_x_above, d_x_below],
    )
    names = ["near", "far", "near17", "far17"]
    return gather_final(
        sums,
        first,
        [exps[name] for name in names],
        [blocks[name] for name in names],
        near_trio,
        far_trio,
    )


def solution(mesh):
    placed = (P(("row", "col"), None), P(("row", "col")))
    return jax.shard_map(
        on_device, mesh=mesh, in_specs=placed, out_specs=P(("row", "col"), None), check_vma=False
    )
```

```python
import functools

import jax
import jax.numpy as jnp
from jax import lax
from jax.experimental import pallas as pl
from jax.experimental.pallas import tpu as pltpu
from jax.sharding import PartitionSpec as P

inverse_temp = 5.0
epsilon = 1e-06
both = ("row", "col")
lanes = 128
chunk = 256


def routes(rows, cols):
    count = rows * cols
    far_step = cols
    x_step = count // 4
    line = cols // 2

    def wrap(value):
        return value % count

    def core(b):
        return (b // cols) % 2

    def half(b):
        return (b // (2 * cols)) % 2

    def far17(b):
        j = b % cols
        if core(b) == 0:
            if j == 0:
                return wrap(b + (2 * cols if half(b) == 0 else -2 * cols) + cols - 1)
            return wrap(b - 2 * cols - 1) if j == cols // 2 else b - 1
        if j == cols - 1:
            return wrap(b + (2 * cols if half(b) == 0 else -2 * cols) - cols + 1)
        return wrap(b + 2 * cols + 1) if j == cols // 2 - 1 else b + 1

    def ring(step):
        return lambda b: b - b % line + (b + step) % line

    def turn(b):
        return wrap(b + 1) if (b + 1) % line == 0 else wrap(b - 1) if b % line == 0 else b

    def turn_source(b):
        taken = turn(b)
        if taken == b:
            return b
        return taken + line - 1 if taken % line == 0 else taken - line + 1

    sources = {
        "even": lambda b: b ^ 1,
        "odd": lambda b: wrap(b - 1 if b % 2 == 0 else b + 1),
        "ring_above": ring(1),
        "ring_below": ring(-1),
        "turn": turn_source,
        "x_even": lambda b: wrap(b + x_step if (b // x_step) % 2 == 0 else b - x_step),
        "x_odd": lambda b: wrap(b - x_step if (b // x_step) % 2 == 0 else b + x_step),
        "x_above": lambda b: wrap(b + x_step),
        "x_below": lambda b: wrap(b - x_step),
        "near": lambda b: b + far_step if core(b) == 0 else b - far_step,
        "far": lambda b: wrap(b - far_step if core(b) == 0 else b + far_step),
        "far17": far17,
    }
    corners = [b for b in range(count) if b % cols == (0, cols - 1)[core(b)] and half(b) == core(b)]
    pairs = {name: [(source(b), b) for b in range(count)] for name, source in sources.items()}
    pairs["corner_down"] = [(s, b) for s, b in pairs["far17"] if b in corners and core(b) == 0]
    pairs["corner_up"] = [(s, b) for s, b in pairs["far17"] if b in corners and core(b) == 1]
    pairs["far17"] = [(s, b) for s, b in pairs["far17"] if b not in corners]
    pairs["row"] = [(b + cols - 1 if b % cols == 0 else b - cols + 1, b) for b in corners]
    pairs["turn"] = [(s, b) for s, b in pairs["turn"] if b not in corners]
    return pairs


vmem_limit = 5 * 1024 * 1024
held = pl.BlockSpec(memory_space=pltpu.VMEM)
small = pl.BlockSpec(memory_space=pltpu.VMEM)
anywhere = pl.BlockSpec(memory_space=pl.ANY)


def hold(*arrays):
    return [pltpu.with_memory_space_constraint(array, pltpu.VMEM) for array in arrays]


def call(kernel, name, in_specs, out_specs, out_shape, flops, moved, exps=0, scratch=()):
    return pl.pallas_call(
        kernel,
        in_specs=in_specs,
        out_specs=out_specs,
        out_shape=out_shape,
        scratch_shapes=scratch,
        compiler_params=pltpu.CompilerParams(vmem_limit_bytes=vmem_limit),
        cost_estimate=pl.CostEstimate(flops=flops, bytes_accessed=moved, transcendentals=exps),
        name=name,
    )


def parts(rows):
    return [slice(start, start + chunk) for start in range(0, rows, chunk)]


def normalize_kernel(rows_ref, out_ref, held_ref, sems):
    rows = rows_ref.shape[0]
    copies = []
    for number, part in enumerate(parts(rows)):
        copy = pltpu.make_async_copy(rows_ref.at[part], held_ref.at[part], sems.at[number])
        copy.start()
        copies.append(copy)
    for copy, part in zip(copies, parts(rows)):
        copy.wait()
        wide = held_ref[part, :].astype(jnp.float32)
        scale = lax.rsqrt(jnp.sum(wide * wide, axis=-1, keepdims=True) + epsilon)
        out_ref[part, :] = (wide * scale).astype(jnp.bfloat16)


def normalize(embeddings):
    rows, width = embeddings.shape
    return call(
        normalize_kernel,
        "normalize",
        [anywhere],
        held,
        pltpu.VMEM((rows, width), jnp.bfloat16),
        4 * rows * width,
        4 * rows * width,
        scratch=[
            pltpu.VMEM((rows, width), jnp.bfloat16),
            pltpu.SemaphoreType.DMA((rows // chunk,)),
        ],
    )(pltpu.with_memory_space_constraint(embeddings, pltpu.HBM))


def exps_of(mine, theirs):
    scores = lax.dot_general(
        mine, theirs, (((1,), (1,)), ((), ())), preferred_element_type=jnp.float32
    )
    return jnp.exp(scores * inverse_temp)


def fold(exps):
    total = exps[:, :lanes]
    for start in range(lanes, exps.shape[1], lanes):
        total = total + exps[:, start : start + lanes]
    return total


def self_kernel(mine_ref, pos_ref, exps_ref, sums_ref, matched_ref):
    rows = mine_ref.shape[0]
    pairs = [pos_ref[number : number + 1, :] for number in range(rows // lanes)]
    partners = jnp.concatenate(pairs, axis=1)
    for part in parts(rows):
        k = lax.broadcasted_iota(jnp.int32, (chunk, rows), 0) + part.start
        j = lax.broadcasted_iota(jnp.int32, (chunk, rows), 1)
        exps = jnp.where(k == j, 0.0, exps_of(mine_ref[part, :], mine_ref[...]))
        exps_ref[part, :] = exps.astype(jnp.bfloat16)
        sums_ref[part, :] = fold(exps)
        picks = jnp.where(k == partners, 1.0, 0.0).astype(jnp.bfloat16)
        matched = jnp.dot(picks, mine_ref[...], preferred_element_type=jnp.float32)
        matched_ref[part, :] = matched.astype(jnp.bfloat16)


def self_tile(normed, positives):
    rows, width = normed.shape
    return call(
        self_kernel,
        "self_tile",
        [held, small],
        [held] * 3,
        [
            pltpu.VMEM((rows, rows), jnp.bfloat16),
            pltpu.VMEM((rows, lanes), jnp.float32),
            pltpu.VMEM((rows, width), jnp.bfloat16),
        ],
        4 * rows * rows * width,
        4 * rows * width + 2 * rows * rows,
        rows * rows,
    )(*hold(normed), positives)


def tile_kernel(mine_ref, theirs_ref, before_ref, exps_ref, sums_ref):
    for part in parts(mine_ref.shape[0]):
        exps = exps_of(mine_ref[part, :], theirs_ref[...])
        exps_ref[part, :] = exps.astype(jnp.bfloat16)
        sums_ref[part, :] = before_ref[part, :] + fold(exps)


def pair_tile(normed, block, sums):
    rows, width = normed.shape
    return call(
        tile_kernel,
        "pair_tile",
        [held] * 3,
        [held] * 2,
        [pltpu.VMEM((rows, rows), jnp.bfloat16), pltpu.VMEM((rows, lanes), jnp.float32)],
        2 * rows * rows * width,
        4 * rows * width + 2 * rows * rows,
        rows * rows,
    )(*hold(normed, block, sums))


def last_kernel(mine_ref, theirs_ref, before_ref, exps_ref, sums_ref, denoms_ref):
    for part in parts(mine_ref.shape[0]):
        exps = exps_of(mine_ref[part, :], theirs_ref[...])
        exps_ref[part, :] = exps.astype(jnp.bfloat16)
        sums = before_ref[part, :] + fold(exps)
        sums_ref[part, :] = sums
        denoms_ref[:, part] = jnp.sum(sums.T, axis=0, keepdims=True)


def last_tile(normed, block, sums):
    rows, width = normed.shape
    return call(
        last_kernel,
        "last_tile",
        [held] * 3,
        [held] * 3,
        [
            pltpu.VMEM((rows, rows), jnp.bfloat16),
            pltpu.VMEM((rows, lanes), jnp.float32),
            pltpu.VMEM((1, rows), jnp.float32),
        ],
        2 * rows * rows * width,
        4 * rows * width + 2 * rows * rows,
        rows * rows,
    )(*hold(normed, block, sums))


def far17_kernel(far_ref, near_ref, mine_ref, out_ref):
    cols, col = lax.axis_size("col"), lax.axis_index("col")
    core0 = lax.axis_index("row") % 2 == 0
    last = col == jnp.where(core0, cols - 1, 0)
    turn = col == jnp.where(core0, cols // 2 - 1, cols // 2)
    for chosen, ref in [(last, mine_ref), (turn, near_ref), (~last & ~turn, far_ref)]:

        @pl.when(chosen)
        def _():
            out_ref[...] = ref[...]


def at_corner():
    cols, row = lax.axis_size("col"), lax.axis_index("row")
    core, half = row % 2, (row // 2) % 2
    return (lax.axis_index("col") == core * (cols - 1)) & (half == core)


def corner_kernel(far17_ref, down_ref, up_ref, out_ref):
    corner = at_corner()
    core0 = lax.axis_index("row") % 2 == 0
    for chosen, ref in [(~corner, far17_ref), (corner & core0, down_ref), (corner & ~core0, up_ref)]:

        @pl.when(chosen)
        def _():
            out_ref[...] = ref[...]


def turn_kernel(above_ref, below_ref, out_ref):
    line = lax.axis_size("col") // 2
    place = lax.axis_index("col") % line

    @pl.when(place == line - 1)
    def _():
        out_ref[...] = above_ref[...]

    @pl.when(place == 0)
    def _():
        out_ref[...] = below_ref[...]


def merge_kernel(shift, core, ring_ref, turn_ref, row_ref, out_ref):
    turns = (lax.axis_index("col") + shift) % (lax.axis_size("col") // 2) == 0
    corner = at_corner() & (lax.axis_index("row") % 2 == core)
    for chosen, ref in [(~turns, ring_ref), (turns & ~corner, turn_ref), (corner, row_ref)]:

        @pl.when(chosen)
        def _():
            out_ref[...] = ref[...]


def near17_kernel(below_ref, above_ref, out_ref):
    core0 = lax.axis_index("row") % 2 == 0

    @pl.when(core0)
    def _():
        out_ref[...] = below_ref[...]

    @pl.when(~core0)
    def _():
        out_ref[...] = above_ref[...]


def choose(kernel, name, *choices):
    shape = choices[0].shape
    return call(
        kernel,
        name,
        [held] * len(choices),
        held,
        pltpu.VMEM(shape, jnp.bfloat16),
        0,
        4 * shape[0] * shape[1],
    )(*hold(*choices))


def weighted(sums_ref, others, exps_refs, block_refs, part):
    mine = 1.0 / jnp.sum(sums_ref[part, :], axis=1, keepdims=True)
    total = None
    for other, exps_ref, block_ref in zip(others, exps_refs, block_refs):
        weights = exps_ref[part, :].astype(jnp.float32) * (mine + other)
        term = jnp.dot(
            weights.astype(jnp.bfloat16), block_ref[...], preferred_element_type=jnp.float32
        )
        total = term if total is None else total + term
    return total


def first_kernel(count, sums_ref, matched_ref, *refs):
    exps_refs, block_refs = refs[:count], refs[count : 2 * count]
    trio_ref, x_even_ref, x_odd_ref, out_ref = refs[2 * count :]
    even = (lax.axis_index("row") // (lax.axis_size("row") // 4)) % 2 == 0
    x_above = jnp.where(even, x_even_ref[...], x_odd_ref[...])
    x_below = jnp.where(even, x_odd_ref[...], x_even_ref[...])
    norms = [trio_ref[0:1, :], trio_ref[1:2, :], trio_ref[2:3, :], x_above, x_below]
    others = [1.0 / norm for norm in norms]
    for part in parts(sums_ref.shape[0]):
        total = weighted(sums_ref, others, exps_refs, block_refs, part)
        out_ref[part, :] = total - 2.0 * matched_ref[part, :].astype(jnp.float32)


def final_kernel(count, sums_ref, first_ref, *refs):
    exps_refs, block_refs = refs[:count], refs[count : 2 * count]
    near_ref, far_ref, out_ref, held_ref, sems = refs[2 * count :]
    core0 = lax.axis_index("row") % 2 == 0
    near17 = jnp.where(core0, near_ref[1:2, :], near_ref[2:3, :])
    far17 = jnp.where(core0, far_ref[2:3, :], far_ref[1:2, :])
    others = [1.0 / norm for norm in (near_ref[0:1, :], far_ref[0:1, :], near17, far17)]
    copies = []
    *most, last = parts(sums_ref.shape[0])
    half = (last.start + last.stop) // 2
    for number, part in enumerate([*most, slice(last.start, half), slice(half, last.stop)]):
        total = weighted(sums_ref, others, exps_refs, block_refs, part)
        held_ref[part, :] = inverse_temp * (first_ref[part, :] + total)
        copy = pltpu.make_async_copy(held_ref.at[part], out_ref.at[part], sems.at[number])
        copy.start()
        copies.append(copy)
    for copy in copies:
        copy.wait()


def gather_first(sums, matched, exps, blocks, norms):
    count, (rows, width) = len(exps), matched.shape
    return call(
        functools.partial(first_kernel, count),
        "gather_first",
        [held] * (2 * count + 5),
        held,
        pltpu.VMEM((rows, width), jnp.float32),
        2 * count * rows * rows * width,
        count * 2 * rows * (rows + width) + 8 * rows * width,
    )(*hold(sums, matched, *exps, *blocks, *norms))


def gather_final(sums, first, exps, blocks, near_trio, far_trio):
    count, (rows, width) = len(exps), first.shape
    return call(
        functools.partial(final_kernel, count),
        "gather_final",
        [held] * (2 * count + 4),
        anywhere,
        jax.ShapeDtypeStruct((rows, width), jnp.float32),
        2 * count * rows * rows * width,
        count * 2 * rows * (rows + width) + 8 * rows * width,
        scratch=[
            pltpu.VMEM((rows, width), jnp.float32),
            pltpu.SemaphoreType.DMA((rows // chunk + 1,)),
        ],
    )(*hold(sums, first, *exps, *blocks, near_trio, far_trio))


def trio_kernel(mine_ref, even_ref, odd_ref, out_ref):
    even = lax.axis_index("col") % 2 == 0
    out_ref[0:1, :] = mine_ref[...]
    out_ref[1:2, :] = jnp.where(even, even_ref[...], odd_ref[...])
    out_ref[2:3, :] = jnp.where(even, odd_ref[...], even_ref[...])


def trio_of(mine, even, odd):
    width = mine.shape[1]
    return call(
        trio_kernel,
        "trio",
        [held] * 3,
        held,
        pltpu.VMEM((3, width), jnp.float32),
        0,
        24 * width,
    )(*hold(mine, even, odd))


def on_device(embeddings, positives):
    rows, cols = lax.axis_size("row"), lax.axis_size("col")
    route = routes(rows, cols)

    def send(block, name):
        return lax.ppermute(block, both, route[name])

    normed = normalize(embeddings)
    near = send(normed, "near")
    ring_above = send(normed, "ring_above")
    ring_below = send(normed, "ring_below")
    far = send(normed, "far")
    self_exps, sums, matched = self_tile(normed, positives.reshape(-1, lanes))
    later, near, sums = lax.optimization_barrier((normed, near, sums))
    x_below = send(later, "x_below")
    x_above = send(later, "x_above")
    ring_above, sums = lax.optimization_barrier((ring_above, sums))
    turn = send(choose(turn_kernel, "turn", ring_above, ring_below), "turn")
    passed = choose(far17_kernel, "far17", far, near, normed)
    far17 = send(passed, "far17")
    across = send(far, "row")
    corner_down = send(x_below, "corner_down")
    corner_up = send(x_above, "corner_up")
    exps, blocks = {}, {}

    def add(sums, **some):
        for name, block in some.items():
            blocks[name] = block
            exps[name], sums = pair_tile(normed, block, sums)
        return sums

    sums = add(sums, near=near, far=far, x_below=x_below, x_above=x_above)
    turn, sums = lax.optimization_barrier((turn, sums))
    above = choose(functools.partial(merge_kernel, 1, 1), "above", ring_above, turn, across)
    below = choose(functools.partial(merge_kernel, 0, 0), "below", ring_below, turn, across)
    near17 = send(choose(near17_kernel, "near17", below, above), "near")
    sums = add(sums, above=above, below=below)
    sums = add(sums, far17=choose(corner_kernel, "corner", far17, corner_down, corner_up))
    blocks["near17"] = near17
    exps["near17"], sums, denoms = last_tile(normed, near17, sums)

    trio = trio_of(denoms, send(denoms, "even"), send(denoms, "odd"))
    d_x_even = send(denoms, "x_even")
    d_x_odd = send(denoms, "x_odd")
    near_trio = send(trio, "near")
    far_trio = send(trio, "far")

    names = ["above", "below", "x_above", "x_below"]
    first = gather_first(
        sums,
        matched,
        [self_exps] + [exps[name] for name in names],
        [normed] + [blocks[name] for name in names],
        [trio, d_x_even, d_x_odd],
    )
    names = ["near", "far", "near17", "far17"]
    return gather_final(
        sums,
        first,
        [exps[name] for name in names],
        [blocks[name] for name in names],
        near_trio,
        far_trio,
    )


def solution(mesh):
    placed = (P(("row", "col"), None), P(("row", "col")))
    return jax.shard_map(
        on_device, mesh=mesh, in_specs=placed, out_specs=P(("row", "col"), None), check_vma=False
    )
```

```python
import functools

import jax
import jax.numpy as jnp
from jax import lax
from jax.experimental import pallas as pl
from jax.experimental.pallas import tpu as pltpu
from jax.sharding import PartitionSpec as P

inverse_temp = 5.0
epsilon = 1e-06
both = ("row", "col")
lanes = 128
chunk = 256


def routes(rows, cols):
    count = rows * cols
    far_step = cols
    x_step = count // 4
    line = cols // 2

    def wrap(value):
        return value % count

    def core(b):
        return (b // cols) % 2

    def half(b):
        return (b // (2 * cols)) % 2

    def far17(b):
        j = b % cols
        if core(b) == 0:
            if j == 0:
                return wrap(b + (2 * cols if half(b) == 0 else -2 * cols) + cols - 1)
            return wrap(b - 2 * cols - 1) if j == cols // 2 else b - 1
        if j == cols - 1:
            return wrap(b + (2 * cols if half(b) == 0 else -2 * cols) - cols + 1)
        return wrap(b + 2 * cols + 1) if j == cols // 2 - 1 else b + 1

    def near(b):
        return b + far_step if core(b) == 0 else b - far_step

    def ring(step):
        return lambda b: b - b % line + (b + step) % line

    def turn(b):
        return wrap(b + 1) if (b + 1) % line == 0 else wrap(b - 1) if b % line == 0 else b

    def turn_source(b):
        taken = turn(b)
        if taken == b:
            return near(b)
        return taken + line - 1 if taken % line == 0 else taken - line + 1

    sources = {
        "even": lambda b: b ^ 1,
        "odd": lambda b: wrap(b - 1 if b % 2 == 0 else b + 1),
        "ring_above": ring(1),
        "ring_below": ring(-1),
        "turn": turn_source,
        "x_even": lambda b: wrap(b + x_step if (b // x_step) % 2 == 0 else b - x_step),
        "x_odd": lambda b: wrap(b - x_step if (b // x_step) % 2 == 0 else b + x_step),
        "x_first": lambda b: wrap(b - x_step if core(b) == 0 else b + x_step),
        "x_second": lambda b: wrap(b + x_step if core(b) == 0 else b - x_step),
        "near": near,
        "far": lambda b: wrap(b - far_step if core(b) == 0 else b + far_step),
        "far17": far17,
    }
    corners = [b for b in range(count) if b % cols == (0, cols - 1)[core(b)] and half(b) == core(b)]
    pairs = {name: [(source(b), b) for b in range(count)] for name, source in sources.items()}
    crossing = {s: b for s, b in pairs["far17"] if b in corners}
    idle = {b: near(b) for b in corners}
    idle.update({b: near(b) for b in range(count) if b not in crossing and b not in corners})
    idle.update(crossing)
    pairs["corner"] = sorted(idle.items())
    pairs["row"] = [(b + cols - 1 if b % cols == 0 else b - cols + 1, b) for b in corners]
    free = {s: near(s) for s, b in pairs["far17"] if b in corners}
    pairs["far17"] = [(s, free.get(s, b)) for s, b in pairs["far17"]]
    free = {s: s + line - 1 if s % line == 0 else s - line + 1 for s, b in pairs["turn"] if b in corners}
    pairs["turn"] = [(s, free.get(s, b)) for s, b in pairs["turn"]]
    return pairs


vmem_limit = 5 * 1024 * 1024
held = pl.BlockSpec(memory_space=pltpu.VMEM)
small = pl.BlockSpec(memory_space=pltpu.VMEM)
anywhere = pl.BlockSpec(memory_space=pl.ANY)


def hold(*arrays):
    return [pltpu.with_memory_space_constraint(array, pltpu.VMEM) for array in arrays]


def call(kernel, name, in_specs, out_specs, out_shape, flops, moved, exps=0, scratch=()):
    return pl.pallas_call(
        kernel,
        in_specs=in_specs,
        out_specs=out_specs,
        out_shape=out_shape,
        scratch_shapes=scratch,
        compiler_params=pltpu.CompilerParams(vmem_limit_bytes=vmem_limit),
        cost_estimate=pl.CostEstimate(flops=flops, bytes_accessed=moved, transcendentals=exps),
        name=name,
    )


def parts(rows):
    return [slice(start, start + chunk) for start in range(0, rows, chunk)]


def normalize_kernel(rows_ref, out_ref, held_ref, sems):
    rows = rows_ref.shape[0]
    copies = []
    for number, part in enumerate(parts(rows)):
        copy = pltpu.make_async_copy(rows_ref.at[part], held_ref.at[part], sems.at[number])
        copy.start()
        copies.append(copy)
    for copy, part in zip(copies, parts(rows)):
        copy.wait()
        wide = held_ref[part, :].astype(jnp.float32)
        scale = lax.rsqrt(jnp.sum(wide * wide, axis=-1, keepdims=True) + epsilon)
        out_ref[part, :] = (wide * scale).astype(jnp.bfloat16)


def normalize(embeddings):
    rows, width = embeddings.shape
    return call(
        normalize_kernel,
        "normalize",
        [anywhere],
        held,
        pltpu.VMEM((rows, width), jnp.bfloat16),
        4 * rows * width,
        4 * rows * width,
        scratch=[
            pltpu.VMEM((rows, width), jnp.bfloat16),
            pltpu.SemaphoreType.DMA((rows // chunk,)),
        ],
    )(pltpu.with_memory_space_constraint(embeddings, pltpu.HBM))


def exps_of(mine, theirs):
    scores = lax.dot_general(
        mine, theirs, (((1,), (1,)), ((), ())), preferred_element_type=jnp.float32
    )
    return jnp.exp(scores * inverse_temp)


def fold(exps):
    total = exps[:, :lanes]
    for start in range(lanes, exps.shape[1], lanes):
        total = total + exps[:, start : start + lanes]
    return total


def self_kernel(mine_ref, pos_ref, exps_ref, sums_ref, matched_ref):
    rows = mine_ref.shape[0]
    pairs = [pos_ref[number : number + 1, :] for number in range(rows // lanes)]
    partners = jnp.concatenate(pairs, axis=1)
    for part in parts(rows):
        k = lax.broadcasted_iota(jnp.int32, (chunk, rows), 0) + part.start
        j = lax.broadcasted_iota(jnp.int32, (chunk, rows), 1)
        exps = jnp.where(k == j, 0.0, exps_of(mine_ref[part, :], mine_ref[...]))
        exps_ref[part, :] = exps.astype(jnp.bfloat16)
        sums_ref[part, :] = fold(exps)
        picks = jnp.where(k == partners, 1.0, 0.0).astype(jnp.bfloat16)
        matched = jnp.dot(picks, mine_ref[...], preferred_element_type=jnp.float32)
        matched_ref[part, :] = matched.astype(jnp.bfloat16)


def self_tile(normed, positives):
    rows, width = normed.shape
    return call(
        self_kernel,
        "self_tile",
        [held, small],
        [held] * 3,
        [
            pltpu.VMEM((rows, rows), jnp.bfloat16),
            pltpu.VMEM((rows, lanes), jnp.float32),
            pltpu.VMEM((rows, width), jnp.bfloat16),
        ],
        4 * rows * rows * width,
        4 * rows * width + 2 * rows * rows,
        rows * rows,
    )(*hold(normed), positives)


def tile_kernel(mine_ref, theirs_ref, before_ref, exps_ref, sums_ref):
    for part in parts(mine_ref.shape[0]):
        exps = exps_of(mine_ref[part, :], theirs_ref[...])
        exps_ref[part, :] = exps.astype(jnp.bfloat16)
        sums_ref[part, :] = before_ref[part, :] + fold(exps)


def pair_tile(normed, block, sums):
    rows, width = normed.shape
    return call(
        tile_kernel,
        "pair_tile",
        [held] * 3,
        [held] * 2,
        [pltpu.VMEM((rows, rows), jnp.bfloat16), pltpu.VMEM((rows, lanes), jnp.float32)],
        2 * rows * rows * width,
        4 * rows * width + 2 * rows * rows,
        rows * rows,
    )(*hold(normed, block, sums))


def last_kernel(mine_ref, theirs_ref, before_ref, exps_ref, sums_ref, denoms_ref):
    for part in parts(mine_ref.shape[0]):
        exps = exps_of(mine_ref[part, :], theirs_ref[...])
        exps_ref[part, :] = exps.astype(jnp.bfloat16)
        sums = before_ref[part, :] + fold(exps)
        sums_ref[part, :] = sums
        denoms_ref[:, part] = jnp.sum(sums.T, axis=0, keepdims=True)


def last_tile(normed, block, sums):
    rows, width = normed.shape
    return call(
        last_kernel,
        "last_tile",
        [held] * 3,
        [held] * 3,
        [
            pltpu.VMEM((rows, rows), jnp.bfloat16),
            pltpu.VMEM((rows, lanes), jnp.float32),
            pltpu.VMEM((1, rows), jnp.float32),
        ],
        2 * rows * rows * width,
        4 * rows * width + 2 * rows * rows,
        rows * rows,
    )(*hold(normed, block, sums))


def far17_kernel(far_ref, near_ref, mine_ref, out_ref):
    cols, col = lax.axis_size("col"), lax.axis_index("col")
    core0 = lax.axis_index("row") % 2 == 0
    last = col == jnp.where(core0, cols - 1, 0)
    turn = col == jnp.where(core0, cols // 2 - 1, cols // 2)
    for chosen, ref in [(last, mine_ref), (turn, near_ref), (~last & ~turn, far_ref)]:

        @pl.when(chosen)
        def _():
            out_ref[...] = ref[...]


def at_corner():
    cols, row = lax.axis_size("col"), lax.axis_index("row")
    core, half = row % 2, (row // 2) % 2
    return (lax.axis_index("col") == core * (cols - 1)) & (half == core)


def corner_kernel(far17_ref, corner_ref, out_ref):
    corner = at_corner()

    @pl.when(corner)
    def _():
        out_ref[...] = corner_ref[...]

    @pl.when(~corner)
    def _():
        out_ref[...] = far17_ref[...]


def turn_kernel(above_ref, below_ref, out_ref):
    line = lax.axis_size("col") // 2
    place = lax.axis_index("col") % line

    @pl.when(place == line - 1)
    def _():
        out_ref[...] = above_ref[...]

    @pl.when(place == 0)
    def _():
        out_ref[...] = below_ref[...]


def merge_kernel(shift, core, ring_ref, turn_ref, row_ref, out_ref):
    turns = (lax.axis_index("col") + shift) % (lax.axis_size("col") // 2) == 0
    corner = at_corner() & (lax.axis_index("row") % 2 == core)
    for chosen, ref in [(~turns, ring_ref), (turns & ~corner, turn_ref), (corner, row_ref)]:

        @pl.when(chosen)
        def _():
            out_ref[...] = ref[...]


def near17_kernel(below_ref, above_ref, out_ref):
    core0 = lax.axis_index("row") % 2 == 0

    @pl.when(core0)
    def _():
        out_ref[...] = below_ref[...]

    @pl.when(~core0)
    def _():
        out_ref[...] = above_ref[...]


def choose(kernel, name, *choices):
    shape = choices[0].shape
    return call(
        kernel,
        name,
        [held] * len(choices),
        held,
        pltpu.VMEM(shape, jnp.bfloat16),
        0,
        4 * shape[0] * shape[1],
    )(*hold(*choices))


def weighted(sums_ref, others, exps_refs, block_refs, part):
    mine = 1.0 / jnp.sum(sums_ref[part, :], axis=1, keepdims=True)
    total = None
    for other, exps_ref, block_ref in zip(others, exps_refs, block_refs):
        weights = exps_ref[part, :].astype(jnp.float32) * (mine + other)
        term = jnp.dot(
            weights.astype(jnp.bfloat16), block_ref[...], preferred_element_type=jnp.float32
        )
        total = term if total is None else total + term
    return total


def first_kernel(count, sums_ref, matched_ref, *refs):
    exps_refs, block_refs = refs[:count], refs[count : 2 * count]
    trio_ref, x_even_ref, x_odd_ref, out_ref = refs[2 * count :]
    row = lax.axis_index("row")
    even = (row // (lax.axis_size("row") // 4)) % 2 == row % 2
    x_first = jnp.where(even, x_odd_ref[...], x_even_ref[...])
    x_second = jnp.where(even, x_even_ref[...], x_odd_ref[...])
    norms = [trio_ref[0:1, :], trio_ref[1:2, :], trio_ref[2:3, :], x_first, x_second]
    others = [1.0 / norm for norm in norms]
    for part in parts(sums_ref.shape[0]):
        total = weighted(sums_ref, others, exps_refs, block_refs, part)
        out_ref[part, :] = total - 2.0 * matched_ref[part, :].astype(jnp.float32)


def final_kernel(count, sums_ref, first_ref, *refs):
    exps_refs, block_refs = refs[:count], refs[count : 2 * count]
    near_ref, far_ref, out_ref, held_ref, sems = refs[2 * count :]
    core0 = lax.axis_index("row") % 2 == 0
    near17 = jnp.where(core0, near_ref[1:2, :], near_ref[2:3, :])
    far17 = jnp.where(core0, far_ref[2:3, :], far_ref[1:2, :])
    others = [1.0 / norm for norm in (near_ref[0:1, :], far_ref[0:1, :], near17, far17)]
    copies = []
    *most, last = parts(sums_ref.shape[0])
    half = (last.start + last.stop) // 2
    for number, part in enumerate([*most, slice(last.start, half), slice(half, last.stop)]):
        total = weighted(sums_ref, others, exps_refs, block_refs, part)
        held_ref[part, :] = inverse_temp * (first_ref[part, :] + total)
        copy = pltpu.make_async_copy(held_ref.at[part], out_ref.at[part], sems.at[number])
        copy.start()
        copies.append(copy)
    for copy in copies:
        copy.wait()


def gather_first(sums, matched, exps, blocks, norms):
    count, (rows, width) = len(exps), matched.shape
    return call(
        functools.partial(first_kernel, count),
        "gather_first",
        [held] * (2 * count + 5),
        held,
        pltpu.VMEM((rows, width), jnp.float32),
        2 * count * rows * rows * width,
        count * 2 * rows * (rows + width) + 8 * rows * width,
    )(*hold(sums, matched, *exps, *blocks, *norms))


def gather_final(sums, first, exps, blocks, near_trio, far_trio):
    count, (rows, width) = len(exps), first.shape
    return call(
        functools.partial(final_kernel, count),
        "gather_final",
        [held] * (2 * count + 4),
        anywhere,
        jax.ShapeDtypeStruct((rows, width), jnp.float32),
        2 * count * rows * rows * width,
        count * 2 * rows * (rows + width) + 8 * rows * width,
        scratch=[
            pltpu.VMEM((rows, width), jnp.float32),
            pltpu.SemaphoreType.DMA((rows // chunk + 1,)),
        ],
    )(*hold(sums, first, *exps, *blocks, near_trio, far_trio))


def trio_kernel(mine_ref, even_ref, odd_ref, out_ref):
    even = lax.axis_index("col") % 2 == 0
    out_ref[0:1, :] = mine_ref[...]
    out_ref[1:2, :] = jnp.where(even, even_ref[...], odd_ref[...])
    out_ref[2:3, :] = jnp.where(even, odd_ref[...], even_ref[...])


def trio_of(mine, even, odd):
    width = mine.shape[1]
    return call(
        trio_kernel,
        "trio",
        [held] * 3,
        held,
        pltpu.VMEM((3, width), jnp.float32),
        0,
        24 * width,
    )(*hold(mine, even, odd))


def on_device(embeddings, positives):
    rows, cols = lax.axis_size("row"), lax.axis_size("col")
    route = routes(rows, cols)

    def send(block, name):
        return lax.ppermute(block, both, route[name])

    normed = normalize(embeddings)
    near = send(normed, "near")
    ring_above = send(normed, "ring_above")
    ring_below = send(normed, "ring_below")
    far = send(normed, "far")
    self_exps, sums, matched = self_tile(normed, positives.reshape(-1, lanes))
    later, near, sums = lax.optimization_barrier((normed, near, sums))
    x_first = send(later, "x_first")
    x_second = send(later, "x_second")
    ring_above, sums = lax.optimization_barrier((ring_above, sums))
    turn = send(choose(turn_kernel, "turn", ring_above, ring_below), "turn")
    passed = choose(far17_kernel, "far17", far, near, normed)
    far17 = send(passed, "far17")
    far, passed = lax.optimization_barrier((far, passed))
    across = send(far, "row")
    corner = send(x_first, "corner")
    exps, blocks = {}, {}

    def add(sums, **some):
        for name, block in some.items():
            blocks[name] = block
            exps[name], sums = pair_tile(normed, block, sums)
        return sums

    sums = add(sums, near=near, far=far, x_first=x_first, x_second=x_second)
    turn, sums = lax.optimization_barrier((turn, sums))
    above = choose(functools.partial(merge_kernel, 1, 1), "above", ring_above, turn, across)
    below = choose(functools.partial(merge_kernel, 0, 0), "below", ring_below, turn, across)
    near17 = send(choose(near17_kernel, "near17", below, above), "near")
    sums = add(sums, above=above, below=below)
    sums = add(sums, far17=choose(corner_kernel, "corner", far17, corner))
    blocks["near17"] = near17
    exps["near17"], sums, denoms = last_tile(normed, near17, sums)

    trio = trio_of(denoms, send(denoms, "even"), send(denoms, "odd"))
    d_x_even = send(denoms, "x_even")
    d_x_odd = send(denoms, "x_odd")
    near_trio = send(trio, "near")
    far_trio = send(trio, "far")

    names = ["above", "below", "x_first", "x_second"]
    first = gather_first(
        sums,
        matched,
        [self_exps] + [exps[name] for name in names],
        [normed] + [blocks[name] for name in names],
        [trio, d_x_even, d_x_odd],
    )
    names = ["near", "far", "near17", "far17"]
    return gather_final(
        sums,
        first,
        [exps[name] for name in names],
        [blocks[name] for name in names],
        near_trio,
        far_trio,
    )


def solution(mesh):
    placed = (P(("row", "col"), None), P(("row", "col")))
    return jax.shard_map(
        on_device, mesh=mesh, in_specs=placed, out_specs=P(("row", "col"), None), check_vma=False
    )
```

```python
import functools

import jax
import jax.numpy as jnp
from jax import lax
from jax.experimental import pallas as pl
from jax.experimental.pallas import tpu as pltpu
from jax.sharding import PartitionSpec as P

inverse_temp = 5.0
epsilon = 1e-06
both = ("row", "col")
lanes = 128
chunk = 256


def routes(rows, cols):
    count = rows * cols
    far_step = cols
    x_step = count // 4
    line = cols // 2

    def wrap(value):
        return value % count

    def core(b):
        return (b // cols) % 2

    def half(b):
        return (b // (2 * cols)) % 2

    def far17(b):
        j = b % cols
        if core(b) == 0:
            if j == 0:
                return wrap(b + (2 * cols if half(b) == 0 else -2 * cols) + cols - 1)
            return wrap(b - 2 * cols - 1) if j == cols // 2 else b - 1
        if j == cols - 1:
            return wrap(b + (2 * cols if half(b) == 0 else -2 * cols) - cols + 1)
        return wrap(b + 2 * cols + 1) if j == cols // 2 - 1 else b + 1

    def near(b):
        return b + far_step if core(b) == 0 else b - far_step

    def ring(step):
        return lambda b: b - b % line + (b + step) % line

    def turn(b):
        return wrap(b + 1) if (b + 1) % line == 0 else wrap(b - 1) if b % line == 0 else b

    def turn_source(b):
        taken = turn(b)
        if taken == b:
            return near(b)
        return taken + line - 1 if taken % line == 0 else taken - line + 1

    sources = {
        "even": lambda b: b ^ 1,
        "odd": lambda b: wrap(b - 1 if b % 2 == 0 else b + 1),
        "ring_above": ring(1),
        "ring_below": ring(-1),
        "turn": turn_source,
        "x_even": lambda b: wrap(b + x_step if (b // x_step) % 2 == 0 else b - x_step),
        "x_odd": lambda b: wrap(b - x_step if (b // x_step) % 2 == 0 else b + x_step),
        "x_first": lambda b: wrap(b - x_step if core(b) == 0 else b + x_step),
        "x_second": lambda b: wrap(b + x_step if core(b) == 0 else b - x_step),
        "near": near,
        "far": lambda b: wrap(b - far_step if core(b) == 0 else b + far_step),
        "far17": far17,
    }
    corners = [b for b in range(count) if b % cols == (0, cols - 1)[core(b)] and half(b) == core(b)]
    pairs = {name: [(source(b), b) for b in range(count)] for name, source in sources.items()}
    crossing = {s: b for s, b in pairs["far17"] if b in corners}
    idle = {b: near(b) for b in corners}
    idle.update({b: near(b) for b in range(count) if b not in crossing and b not in corners})
    idle.update(crossing)
    pairs["corner"] = sorted(idle.items())
    pairs["row"] = [(b + cols - 1 if b % cols == 0 else b - cols + 1, b) for b in corners]
    free = {s: near(s) for s, b in pairs["far17"] if b in corners}
    pairs["far17"] = [(s, free.get(s, b)) for s, b in pairs["far17"]]
    free = {s: s + line - 1 if s % line == 0 else s - line + 1 for s, b in pairs["turn"] if b in corners}
    pairs["turn"] = [(s, free.get(s, b)) for s, b in pairs["turn"]]
    return pairs


vmem_limit = 5 * 1024 * 1024
held = pl.BlockSpec(memory_space=pltpu.VMEM)
small = pl.BlockSpec(memory_space=pltpu.VMEM)
anywhere = pl.BlockSpec(memory_space=pl.ANY)


def hold(*arrays):
    return [pltpu.with_memory_space_constraint(array, pltpu.VMEM) for array in arrays]


def call(kernel, name, in_specs, out_specs, out_shape, flops, moved, exps=0, scratch=()):
    return pl.pallas_call(
        kernel,
        in_specs=in_specs,
        out_specs=out_specs,
        out_shape=out_shape,
        scratch_shapes=scratch,
        compiler_params=pltpu.CompilerParams(vmem_limit_bytes=vmem_limit),
        cost_estimate=pl.CostEstimate(flops=flops, bytes_accessed=moved, transcendentals=exps),
        name=name,
    )


def parts(rows):
    return [slice(start, start + chunk) for start in range(0, rows, chunk)]


def normalize_kernel(rows_ref, out_ref, held_ref, sems):
    rows = rows_ref.shape[0]
    copies = []
    for number, part in enumerate(parts(rows)):
        copy = pltpu.make_async_copy(rows_ref.at[part], held_ref.at[part], sems.at[number])
        copy.start()
        copies.append(copy)
    for copy, part in zip(copies, parts(rows)):
        copy.wait()
        wide = held_ref[part, :].astype(jnp.float32)
        scale = lax.rsqrt(jnp.sum(wide * wide, axis=-1, keepdims=True) + epsilon)
        out_ref[part, :] = (wide * scale).astype(jnp.bfloat16)


def normalize(embeddings):
    rows, width = embeddings.shape
    return call(
        normalize_kernel,
        "normalize",
        [anywhere],
        held,
        pltpu.VMEM((rows, width), jnp.bfloat16),
        4 * rows * width,
        4 * rows * width,
        scratch=[
            pltpu.VMEM((rows, width), jnp.bfloat16),
            pltpu.SemaphoreType.DMA((rows // chunk,)),
        ],
    )(pltpu.with_memory_space_constraint(embeddings, pltpu.HBM))


def exps_of(mine, theirs):
    scores = lax.dot_general(
        mine, theirs, (((1,), (1,)), ((), ())), preferred_element_type=jnp.float32
    )
    return jnp.exp(scores * inverse_temp)


def fold(exps):
    total = exps[:, :lanes]
    for start in range(lanes, exps.shape[1], lanes):
        total = total + exps[:, start : start + lanes]
    return total


def self_kernel(mine_ref, pos_ref, exps_ref, sums_ref, matched_ref):
    rows = mine_ref.shape[0]
    pairs = [pos_ref[number : number + 1, :] for number in range(rows // lanes)]
    partners = jnp.concatenate(pairs, axis=1)
    for part in parts(rows):
        k = lax.broadcasted_iota(jnp.int32, (chunk, rows), 0) + part.start
        j = lax.broadcasted_iota(jnp.int32, (chunk, rows), 1)
        exps = jnp.where(k == j, 0.0, exps_of(mine_ref[part, :], mine_ref[...]))
        exps_ref[part, :] = exps.astype(jnp.bfloat16)
        sums_ref[part, :] = fold(exps)
        picks = jnp.where(k == partners, 1.0, 0.0).astype(jnp.bfloat16)
        matched = jnp.dot(picks, mine_ref[...], preferred_element_type=jnp.float32)
        matched_ref[part, :] = matched.astype(jnp.bfloat16)


def self_tile(normed, positives):
    rows, width = normed.shape
    return call(
        self_kernel,
        "self_tile",
        [held, small],
        [held] * 3,
        [
            pltpu.VMEM((rows, rows), jnp.bfloat16),
            pltpu.VMEM((rows, lanes), jnp.float32),
            pltpu.VMEM((rows, width), jnp.bfloat16),
        ],
        4 * rows * rows * width,
        4 * rows * width + 2 * rows * rows,
        rows * rows,
    )(*hold(normed), positives)


def tile_kernel(mine_ref, theirs_ref, before_ref, exps_ref, sums_ref):
    for part in parts(mine_ref.shape[0]):
        exps = exps_of(mine_ref[part, :], theirs_ref[...])
        exps_ref[part, :] = exps.astype(jnp.bfloat16)
        sums_ref[part, :] = before_ref[part, :] + fold(exps)


def pair_tile(normed, block, sums):
    rows, width = normed.shape
    return call(
        tile_kernel,
        "pair_tile",
        [held] * 3,
        [held] * 2,
        [pltpu.VMEM((rows, rows), jnp.bfloat16), pltpu.VMEM((rows, lanes), jnp.float32)],
        2 * rows * rows * width,
        4 * rows * width + 2 * rows * rows,
        rows * rows,
    )(*hold(normed, block, sums))


def last_kernel(mine_ref, theirs_ref, before_ref, exps_ref, sums_ref, denoms_ref):
    for part in parts(mine_ref.shape[0]):
        exps = exps_of(mine_ref[part, :], theirs_ref[...])
        exps_ref[part, :] = exps.astype(jnp.bfloat16)
        sums = before_ref[part, :] + fold(exps)
        sums_ref[part, :] = sums
        denoms_ref[:, part] = jnp.sum(sums.T, axis=0, keepdims=True)


def last_tile(normed, block, sums):
    rows, width = normed.shape
    return call(
        last_kernel,
        "last_tile",
        [held] * 3,
        [held] * 3,
        [
            pltpu.VMEM((rows, rows), jnp.bfloat16),
            pltpu.VMEM((rows, lanes), jnp.float32),
            pltpu.VMEM((1, rows), jnp.float32),
        ],
        2 * rows * rows * width,
        4 * rows * width + 2 * rows * rows,
        rows * rows,
    )(*hold(normed, block, sums))


def far17_kernel(far_ref, near_ref, mine_ref, out_ref):
    cols, col = lax.axis_size("col"), lax.axis_index("col")
    core0 = lax.axis_index("row") % 2 == 0
    last = col == jnp.where(core0, cols - 1, 0)
    turn = col == jnp.where(core0, cols // 2 - 1, cols // 2)
    for chosen, ref in [(last, mine_ref), (turn, near_ref), (~last & ~turn, far_ref)]:

        @pl.when(chosen)
        def _():
            out_ref[...] = ref[...]


def at_corner():
    cols, row = lax.axis_size("col"), lax.axis_index("row")
    core, half = row % 2, (row // 2) % 2
    return (lax.axis_index("col") == core * (cols - 1)) & (half == core)


def corner_kernel(far17_ref, corner_ref, out_ref):
    corner = at_corner()

    @pl.when(corner)
    def _():
        out_ref[...] = corner_ref[...]

    @pl.when(~corner)
    def _():
        out_ref[...] = far17_ref[...]


def turn_kernel(below_ref, above_ref, out_ref):
    line = lax.axis_size("col") // 2
    place = lax.axis_index("col") % line

    @pl.when(place == line - 1)
    def _():
        out_ref[...] = above_ref[...]

    @pl.when(place == 0)
    def _():
        out_ref[...] = below_ref[...]


def merge_kernel(shift, core, ring_ref, turn_ref, row_ref, out_ref):
    turns = (lax.axis_index("col") + shift) % (lax.axis_size("col") // 2) == 0
    corner = at_corner() & (lax.axis_index("row") % 2 == core)
    for chosen, ref in [(~turns, ring_ref), (turns & ~corner, turn_ref), (corner, row_ref)]:

        @pl.when(chosen)
        def _():
            out_ref[...] = ref[...]


def near17_kernel(below_ref, above_ref, out_ref):
    core0 = lax.axis_index("row") % 2 == 0

    @pl.when(core0)
    def _():
        out_ref[...] = below_ref[...]

    @pl.when(~core0)
    def _():
        out_ref[...] = above_ref[...]


def choose(kernel, name, *choices):
    shape = choices[0].shape
    return call(
        kernel,
        name,
        [held] * len(choices),
        held,
        pltpu.VMEM(shape, jnp.bfloat16),
        0,
        4 * shape[0] * shape[1],
    )(*hold(*choices))


def weighted(sums_ref, others, exps_refs, block_refs, part):
    mine = 1.0 / jnp.sum(sums_ref[part, :], axis=1, keepdims=True)
    total = None
    for other, exps_ref, block_ref in zip(others, exps_refs, block_refs):
        weights = exps_ref[part, :].astype(jnp.float32) * (mine + other)
        term = jnp.dot(
            weights.astype(jnp.bfloat16), block_ref[...], preferred_element_type=jnp.float32
        )
        total = term if total is None else total + term
    return total


def first_kernel(count, sums_ref, matched_ref, *refs):
    exps_refs, block_refs = refs[:count], refs[count : 2 * count]
    trio_ref, x_even_ref, x_odd_ref, out_ref = refs[2 * count :]
    row = lax.axis_index("row")
    even = (row // (lax.axis_size("row") // 4)) % 2 == row % 2
    x_first = jnp.where(even, x_odd_ref[...], x_even_ref[...])
    x_second = jnp.where(even, x_even_ref[...], x_odd_ref[...])
    norms = [trio_ref[0:1, :], trio_ref[1:2, :], trio_ref[2:3, :], x_first, x_second]
    others = [1.0 / norm for norm in norms]
    for part in parts(sums_ref.shape[0]):
        total = weighted(sums_ref, others, exps_refs, block_refs, part)
        out_ref[part, :] = total - 2.0 * matched_ref[part, :].astype(jnp.float32)


def final_kernel(count, sums_ref, first_ref, *refs):
    exps_refs, block_refs = refs[:count], refs[count : 2 * count]
    near_ref, far_ref, out_ref, held_ref, sems = refs[2 * count :]
    core0 = lax.axis_index("row") % 2 == 0
    near17 = jnp.where(core0, near_ref[1:2, :], near_ref[2:3, :])
    far17 = jnp.where(core0, far_ref[2:3, :], far_ref[1:2, :])
    others = [1.0 / norm for norm in (near_ref[0:1, :], far_ref[0:1, :], near17, far17)]
    copies = []
    *most, last = parts(sums_ref.shape[0])
    half = (last.start + last.stop) // 2
    for number, part in enumerate([*most, slice(last.start, half), slice(half, last.stop)]):
        total = weighted(sums_ref, others, exps_refs, block_refs, part)
        held_ref[part, :] = inverse_temp * (first_ref[part, :] + total)
        copy = pltpu.make_async_copy(held_ref.at[part], out_ref.at[part], sems.at[number])
        copy.start()
        copies.append(copy)
    for copy in copies:
        copy.wait()


def gather_first(sums, matched, exps, blocks, norms):
    count, (rows, width) = len(exps), matched.shape
    return call(
        functools.partial(first_kernel, count),
        "gather_first",
        [held] * (2 * count + 5),
        held,
        pltpu.VMEM((rows, width), jnp.float32),
        2 * count * rows * rows * width,
        count * 2 * rows * (rows + width) + 8 * rows * width,
    )(*hold(sums, matched, *exps, *blocks, *norms))


def gather_final(sums, first, exps, blocks, near_trio, far_trio):
    count, (rows, width) = len(exps), first.shape
    return call(
        functools.partial(final_kernel, count),
        "gather_final",
        [held] * (2 * count + 4),
        anywhere,
        jax.ShapeDtypeStruct((rows, width), jnp.float32),
        2 * count * rows * rows * width,
        count * 2 * rows * (rows + width) + 8 * rows * width,
        scratch=[
            pltpu.VMEM((rows, width), jnp.float32),
            pltpu.SemaphoreType.DMA((rows // chunk + 1,)),
        ],
    )(*hold(sums, first, *exps, *blocks, near_trio, far_trio))


def trio_kernel(mine_ref, even_ref, odd_ref, out_ref):
    even = lax.axis_index("col") % 2 == 0
    out_ref[0:1, :] = mine_ref[...]
    out_ref[1:2, :] = jnp.where(even, even_ref[...], odd_ref[...])
    out_ref[2:3, :] = jnp.where(even, odd_ref[...], even_ref[...])


def trio_of(mine, even, odd):
    width = mine.shape[1]
    return call(
        trio_kernel,
        "trio",
        [held] * 3,
        held,
        pltpu.VMEM((3, width), jnp.float32),
        0,
        24 * width,
    )(*hold(mine, even, odd))


def on_device(embeddings, positives):
    rows, cols = lax.axis_size("row"), lax.axis_size("col")
    route = routes(rows, cols)

    def send(block, name):
        return lax.ppermute(block, both, route[name])

    normed = normalize(embeddings)
    near = send(normed, "near")
    ring_below = send(normed, "ring_below")
    ring_above = send(normed, "ring_above")
    far = send(normed, "far")
    self_exps, sums, matched = self_tile(normed, positives.reshape(-1, lanes))
    later, near, sums = lax.optimization_barrier((normed, near, sums))
    x_first = send(later, "x_first")
    x_second = send(later, "x_second")
    ring_below, sums = lax.optimization_barrier((ring_below, sums))
    turn = send(choose(turn_kernel, "turn", ring_below, ring_above), "turn")
    passed = choose(far17_kernel, "far17", far, near, normed)
    far17 = send(passed, "far17")
    far, passed = lax.optimization_barrier((far, passed))
    across = send(far, "row")
    corner = send(x_first, "corner")
    exps, blocks = {}, {}

    def add(sums, **some):
        for name, block in some.items():
            blocks[name] = block
            exps[name], sums = pair_tile(normed, block, sums)
        return sums

    sums = add(sums, near=near, far=far, x_first=x_first, x_second=x_second)
    turn, sums = lax.optimization_barrier((turn, sums))
    above = choose(functools.partial(merge_kernel, 1, 1), "above", ring_above, turn, across)
    below = choose(functools.partial(merge_kernel, 0, 0), "below", ring_below, turn, across)
    near17 = send(choose(near17_kernel, "near17", below, above), "near")
    sums = add(sums, above=above, below=below)
    sums = add(sums, far17=choose(corner_kernel, "corner", far17, corner))
    blocks["near17"] = near17
    exps["near17"], sums, denoms = last_tile(normed, near17, sums)

    trio = trio_of(denoms, send(denoms, "even"), send(denoms, "odd"))
    d_x_even = send(denoms, "x_even")
    d_x_odd = send(denoms, "x_odd")
    near_trio = send(trio, "near")
    far_trio = send(trio, "far")

    names = ["above", "below", "x_first", "x_second"]
    first = gather_first(
        sums,
        matched,
        [self_exps] + [exps[name] for name in names],
        [normed] + [blocks[name] for name in names],
        [trio, d_x_even, d_x_odd],
    )
    names = ["near", "far", "near17", "far17"]
    return gather_final(
        sums,
        first,
        [exps[name] for name in names],
        [blocks[name] for name in names],
        near_trio,
        far_trio,
    )


def solution(mesh):
    placed = (P(("row", "col"), None), P(("row", "col")))
    return jax.shard_map(
        on_device, mesh=mesh, in_specs=placed, out_specs=P(("row", "col"), None), check_vma=False
    )
```

```python
import functools

import jax
import jax.numpy as jnp
from jax import lax
from jax.experimental import pallas as pl
from jax.experimental.pallas import tpu as pltpu
from jax.sharding import PartitionSpec as P

inverse_temp = 5.0
epsilon = 1e-06
both = ("row", "col")
lanes = 128
chunk = 256


def routes(rows, cols):
    count = rows * cols
    far_step = cols
    x_step = count // 4
    line = cols // 2

    def wrap(value):
        return value % count

    def core(b):
        return (b // cols) % 2

    def half(b):
        return (b // (2 * cols)) % 2

    def far17(b):
        j = b % cols
        if core(b) == 0:
            if j == 0:
                return wrap(b + (2 * cols if half(b) == 0 else -2 * cols) + cols - 1)
            return wrap(b - 2 * cols - 1) if j == cols // 2 else b - 1
        if j == cols - 1:
            return wrap(b + (2 * cols if half(b) == 0 else -2 * cols) - cols + 1)
        return wrap(b + 2 * cols + 1) if j == cols // 2 - 1 else b + 1

    def near(b):
        return b + far_step if core(b) == 0 else b - far_step

    def ring(step):
        return lambda b: b - b % line + (b + step) % line

    def turn(b):
        return wrap(b + 1) if (b + 1) % line == 0 else wrap(b - 1) if b % line == 0 else b

    def turn_source(b):
        taken = turn(b)
        if taken == b:
            return near(b)
        return taken + line - 1 if taken % line == 0 else taken - line + 1

    sources = {
        "even": lambda b: b ^ 1,
        "odd": lambda b: wrap(b - 1 if b % 2 == 0 else b + 1),
        "ring_above": ring(1),
        "ring_below": ring(-1),
        "turn": turn_source,
        "x_even": lambda b: wrap(b + x_step if (b // x_step) % 2 == 0 else b - x_step),
        "x_odd": lambda b: wrap(b - x_step if (b // x_step) % 2 == 0 else b + x_step),
        "x_first": lambda b: wrap(b - x_step if core(b) == 0 else b + x_step),
        "x_second": lambda b: wrap(b + x_step if core(b) == 0 else b - x_step),
        "near": near,
        "far": lambda b: wrap(b - far_step if core(b) == 0 else b + far_step),
        "far17": far17,
    }
    corners = [b for b in range(count) if b % cols == (0, cols - 1)[core(b)] and half(b) == core(b)]
    pairs = {name: [(source(b), b) for b in range(count)] for name, source in sources.items()}
    crossing = {s: b for s, b in pairs["far17"] if b in corners}
    idle = {b: near(b) for b in corners}
    idle.update({b: near(b) for b in range(count) if b not in crossing and b not in corners})
    idle.update(crossing)
    pairs["corner"] = sorted(idle.items())
    pairs["row"] = [(b + cols - 1 if b % cols == 0 else b - cols + 1, b) for b in corners]
    free = {s: near(s) for s, b in pairs["far17"] if b in corners}
    pairs["far17"] = [(s, free.get(s, b)) for s, b in pairs["far17"]]
    free = {s: s + line - 1 if s % line == 0 else s - line + 1 for s, b in pairs["turn"] if b in corners}
    pairs["turn"] = [(s, free.get(s, b)) for s, b in pairs["turn"]]
    return pairs


vmem_limit = 5 * 1024 * 1024
held = pl.BlockSpec(memory_space=pltpu.VMEM)
small = pl.BlockSpec(memory_space=pltpu.VMEM)
anywhere = pl.BlockSpec(memory_space=pl.ANY)


def hold(*arrays):
    return [pltpu.with_memory_space_constraint(array, pltpu.VMEM) for array in arrays]


def call(kernel, name, in_specs, out_specs, out_shape, flops, moved, exps=0, scratch=(), aliases={}):
    return pl.pallas_call(
        kernel,
        in_specs=in_specs,
        out_specs=out_specs,
        out_shape=out_shape,
        scratch_shapes=scratch,
        input_output_aliases=aliases,
        compiler_params=pltpu.CompilerParams(vmem_limit_bytes=vmem_limit),
        cost_estimate=pl.CostEstimate(flops=flops, bytes_accessed=moved, transcendentals=exps),
        name=name,
    )


def parts(rows):
    return [slice(start, start + chunk) for start in range(0, rows, chunk)]


def normalize_kernel(rows_ref, out_ref, held_ref, sems):
    rows = rows_ref.shape[0]
    copies = []
    for number, part in enumerate(parts(rows)):
        copy = pltpu.make_async_copy(rows_ref.at[part], held_ref.at[part], sems.at[number])
        copy.start()
        copies.append(copy)
    for copy, part in zip(copies, parts(rows)):
        copy.wait()
        wide = held_ref[part, :].astype(jnp.float32)
        scale = lax.rsqrt(jnp.sum(wide * wide, axis=-1, keepdims=True) + epsilon)
        out_ref[part, :] = (wide * scale).astype(jnp.bfloat16)


def normalize(embeddings):
    rows, width = embeddings.shape
    return call(
        normalize_kernel,
        "normalize",
        [anywhere],
        held,
        pltpu.VMEM((rows, width), jnp.bfloat16),
        4 * rows * width,
        4 * rows * width,
        scratch=[
            pltpu.VMEM((rows, width), jnp.bfloat16),
            pltpu.SemaphoreType.DMA((rows // chunk,)),
        ],
    )(pltpu.with_memory_space_constraint(embeddings, pltpu.HBM))


def exps_of(mine, theirs):
    scores = lax.dot_general(
        mine, theirs, (((1,), (1,)), ((), ())), preferred_element_type=jnp.float32
    )
    return jnp.exp(scores * inverse_temp)


def fold(exps):
    total = exps[:, :lanes]
    for start in range(lanes, exps.shape[1], lanes):
        total = total + exps[:, start : start + lanes]
    return total


def self_kernel(mine_ref, pos_ref, exps_ref, sums_ref, matched_ref):
    rows = mine_ref.shape[0]
    pairs = [pos_ref[number : number + 1, :] for number in range(rows // lanes)]
    partners = jnp.concatenate(pairs, axis=1)
    for part in parts(rows):
        k = lax.broadcasted_iota(jnp.int32, (chunk, rows), 0) + part.start
        j = lax.broadcasted_iota(jnp.int32, (chunk, rows), 1)
        exps = jnp.where(k == j, 0.0, exps_of(mine_ref[part, :], mine_ref[...]))
        exps_ref[part, :] = exps.astype(jnp.bfloat16)
        sums_ref[part, :] = fold(exps)
        picks = jnp.where(k == partners, 1.0, 0.0).astype(jnp.bfloat16)
        matched = jnp.dot(picks, mine_ref[...], preferred_element_type=jnp.float32)
        matched_ref[part, :] = matched.astype(jnp.bfloat16)


def self_tile(normed, positives):
    rows, width = normed.shape
    return call(
        self_kernel,
        "self_tile",
        [held, small],
        [held] * 3,
        [
            pltpu.VMEM((rows, rows), jnp.bfloat16),
            pltpu.VMEM((rows, lanes), jnp.float32),
            pltpu.VMEM((rows, width), jnp.bfloat16),
        ],
        4 * rows * rows * width,
        4 * rows * width + 2 * rows * rows,
        rows * rows,
    )(*hold(normed), positives)


def tile_kernel(mine_ref, theirs_ref, before_ref, exps_ref, sums_ref):
    for part in parts(mine_ref.shape[0]):
        exps = exps_of(mine_ref[part, :], theirs_ref[...])
        exps_ref[part, :] = exps.astype(jnp.bfloat16)
        sums_ref[part, :] = before_ref[part, :] + fold(exps)


def pair_tile(normed, block, sums):
    rows, width = normed.shape
    return call(
        tile_kernel,
        "pair_tile",
        [held] * 3,
        [held] * 2,
        [pltpu.VMEM((rows, rows), jnp.bfloat16), pltpu.VMEM((rows, lanes), jnp.float32)],
        2 * rows * rows * width,
        4 * rows * width + 2 * rows * rows,
        rows * rows,
    )(*hold(normed, block, sums))


def last_kernel(mine_ref, theirs_ref, before_ref, exps_ref, sums_ref, denoms_ref):
    for part in parts(mine_ref.shape[0]):
        exps = exps_of(mine_ref[part, :], theirs_ref[...])
        exps_ref[part, :] = exps.astype(jnp.bfloat16)
        sums = before_ref[part, :] + fold(exps)
        sums_ref[part, :] = sums
        denoms_ref[:, part] = jnp.sum(sums.T, axis=0, keepdims=True)


def last_tile(normed, block, sums):
    rows, width = normed.shape
    return call(
        last_kernel,
        "last_tile",
        [held] * 3,
        [held] * 3,
        [
            pltpu.VMEM((rows, rows), jnp.bfloat16),
            pltpu.VMEM((rows, lanes), jnp.float32),
            pltpu.VMEM((1, rows), jnp.float32),
        ],
        2 * rows * rows * width,
        4 * rows * width + 2 * rows * rows,
        rows * rows,
    )(*hold(normed, block, sums))


def far17_kernel(far_ref, near_ref, mine_ref, out_ref):
    cols, col = lax.axis_size("col"), lax.axis_index("col")
    core0 = lax.axis_index("row") % 2 == 0
    last = col == jnp.where(core0, cols - 1, 0)
    turn = col == jnp.where(core0, cols // 2 - 1, cols // 2)
    for chosen, ref in [(last, mine_ref), (turn, near_ref), (~last & ~turn, far_ref)]:

        @pl.when(chosen)
        def _():
            out_ref[...] = ref[...]


def at_corner():
    cols, row = lax.axis_size("col"), lax.axis_index("row")
    core, half = row % 2, (row // 2) % 2
    return (lax.axis_index("col") == core * (cols - 1)) & (half == core)


def corner_kernel(far17_ref, corner_ref, out_ref):
    del far17_ref

    @pl.when(at_corner())
    def _():
        out_ref[...] = corner_ref[...]


def turn_kernel(below_ref, above_ref, out_ref):
    line = lax.axis_size("col") // 2
    place = lax.axis_index("col") % line

    @pl.when(place == line - 1)
    def _():
        out_ref[...] = above_ref[...]

    @pl.when(place == 0)
    def _():
        out_ref[...] = below_ref[...]


def merge_kernel(shift, core, ring_ref, turn_ref, row_ref, out_ref):
    turns = (lax.axis_index("col") + shift) % (lax.axis_size("col") // 2) == 0
    corner = at_corner() & (lax.axis_index("row") % 2 == core)
    for chosen, ref in [(~turns, ring_ref), (turns & ~corner, turn_ref), (corner, row_ref)]:

        @pl.when(chosen)
        def _():
            out_ref[...] = ref[...]


def near17_kernel(below_ref, above_ref, out_ref):
    core0 = lax.axis_index("row") % 2 == 0

    @pl.when(core0)
    def _():
        out_ref[...] = below_ref[...]

    @pl.when(~core0)
    def _():
        out_ref[...] = above_ref[...]


def choose(kernel, name, *choices, aliases={}):
    shape = choices[0].shape
    return call(
        kernel,
        name,
        [held] * len(choices),
        held,
        pltpu.VMEM(shape, jnp.bfloat16),
        0,
        4 * shape[0] * shape[1],
        aliases=aliases,
    )(*hold(*choices))


def weighted(sums_ref, others, exps_refs, block_refs, part):
    mine = 1.0 / jnp.sum(sums_ref[part, :], axis=1, keepdims=True)
    total = None
    for other, exps_ref, block_ref in zip(others, exps_refs, block_refs):
        weights = exps_ref[part, :].astype(jnp.float32) * (mine + other)
        term = jnp.dot(
            weights.astype(jnp.bfloat16), block_ref[...], preferred_element_type=jnp.float32
        )
        total = term if total is None else total + term
    return total


def first_kernel(count, sums_ref, matched_ref, *refs):
    exps_refs, block_refs = refs[:count], refs[count : 2 * count]
    trio_ref, x_even_ref, x_odd_ref, out_ref = refs[2 * count :]
    row = lax.axis_index("row")
    even = (row // (lax.axis_size("row") // 4)) % 2 == row % 2
    x_first = jnp.where(even, x_odd_ref[...], x_even_ref[...])
    x_second = jnp.where(even, x_even_ref[...], x_odd_ref[...])
    norms = [trio_ref[0:1, :], trio_ref[1:2, :], trio_ref[2:3, :], x_first, x_second]
    others = [1.0 / norm for norm in norms]
    for part in parts(sums_ref.shape[0]):
        total = weighted(sums_ref, others, exps_refs, block_refs, part)
        out_ref[part, :] = total - 2.0 * matched_ref[part, :].astype(jnp.float32)


def final_kernel(count, sums_ref, first_ref, *refs):
    exps_refs, block_refs = refs[:count], refs[count : 2 * count]
    far_ref, near_ref, out_ref, held_ref, sems = refs[2 * count :]
    core0 = lax.axis_index("row") % 2 == 0
    near17 = jnp.where(core0, near_ref[1:2, :], near_ref[2:3, :])
    far17 = jnp.where(core0, far_ref[2:3, :], far_ref[1:2, :])
    others = [1.0 / norm for norm in (near_ref[0:1, :], far_ref[0:1, :], near17, far17)]
    copies = []
    *most, last = parts(sums_ref.shape[0])
    half = (last.start + last.stop) // 2
    for number, part in enumerate([*most, slice(last.start, half), slice(half, last.stop)]):
        total = weighted(sums_ref, others, exps_refs, block_refs, part)
        held_ref[part, :] = inverse_temp * (first_ref[part, :] + total)
        copy = pltpu.make_async_copy(held_ref.at[part], out_ref.at[part], sems.at[number])
        copy.start()
        copies.append(copy)
    for copy in copies:
        copy.wait()


def gather_first(sums, matched, exps, blocks, norms):
    count, (rows, width) = len(exps), matched.shape
    return call(
        functools.partial(first_kernel, count),
        "gather_first",
        [held] * (2 * count + 5),
        held,
        pltpu.VMEM((rows, width), jnp.float32),
        2 * count * rows * rows * width,
        count * 2 * rows * (rows + width) + 8 * rows * width,
    )(*hold(sums, matched, *exps, *blocks, *norms))


def gather_final(sums, first, exps, blocks, far_trio, near_trio):
    count, (rows, width) = len(exps), first.shape
    return call(
        functools.partial(final_kernel, count),
        "gather_final",
        [held] * (2 * count + 4),
        anywhere,
        jax.ShapeDtypeStruct((rows, width), jnp.float32),
        2 * count * rows * rows * width,
        count * 2 * rows * (rows + width) + 8 * rows * width,
        scratch=[
            pltpu.VMEM((rows, width), jnp.float32),
            pltpu.SemaphoreType.DMA((rows // chunk + 1,)),
        ],
    )(*hold(sums, first, *exps, *blocks, far_trio, near_trio))


def trio_kernel(mine_ref, odd_ref, even_ref, out_ref):
    even = lax.axis_index("col") % 2 == 0
    out_ref[0:1, :] = mine_ref[...]
    out_ref[1:2, :] = jnp.where(even, even_ref[...], odd_ref[...])
    out_ref[2:3, :] = jnp.where(even, odd_ref[...], even_ref[...])


def trio_of(mine, odd, even):
    width = mine.shape[1]
    return call(
        trio_kernel,
        "trio",
        [held] * 3,
        held,
        pltpu.VMEM((3, width), jnp.float32),
        0,
        24 * width,
    )(*hold(mine, odd, even))


def on_device(embeddings, positives):
    rows, cols = lax.axis_size("row"), lax.axis_size("col")
    route = routes(rows, cols)

    def send(block, name):
        return lax.ppermute(block, both, route[name])

    normed = normalize(embeddings)
    near = send(normed, "near")
    ring_below = send(normed, "ring_below")
    ring_above = send(normed, "ring_above")
    far = send(normed, "far")
    self_exps, sums, matched = self_tile(normed, positives.reshape(-1, lanes))
    later, near, sums = lax.optimization_barrier((normed, near, sums))
    x_first = send(later, "x_first")
    x_second = send(later, "x_second")
    ring_below, sums = lax.optimization_barrier((ring_below, sums))
    turn = send(choose(turn_kernel, "turn", ring_below, ring_above), "turn")
    passed = choose(far17_kernel, "far17", far, near, normed)
    far17 = send(passed, "far17")
    far, passed = lax.optimization_barrier((far, passed))
    across = send(far, "row")
    corner = send(x_first, "corner")
    exps, blocks = {}, {}

    def add(sums, **some):
        for name, block in some.items():
            blocks[name] = block
            exps[name], sums = pair_tile(normed, block, sums)
        return sums

    sums = add(sums, near=near, far=far, x_first=x_first, x_second=x_second)
    turn, sums = lax.optimization_barrier((turn, sums))
    above = choose(functools.partial(merge_kernel, 1, 1), "above", ring_above, turn, across)
    below = choose(functools.partial(merge_kernel, 0, 0), "below", ring_below, turn, across)
    near17 = send(choose(near17_kernel, "near17", below, above), "near")
    sums = add(sums, above=above, below=below)
    sums = add(sums, far17=choose(corner_kernel, "corner", far17, corner, aliases={0: 0}))
    blocks["near17"] = near17
    exps["near17"], sums, denoms = last_tile(normed, near17, sums)

    trio = trio_of(denoms, send(denoms, "odd"), send(denoms, "even"))
    d_x_even = send(denoms, "x_even")
    d_x_odd = send(denoms, "x_odd")
    far_trio = send(trio, "far")
    near_trio = send(trio, "near")

    names = ["above", "below", "x_first", "x_second"]
    first = gather_first(
        sums,
        matched,
        [self_exps] + [exps[name] for name in names],
        [normed] + [blocks[name] for name in names],
        [trio, d_x_even, d_x_odd],
    )
    names = ["near", "far", "near17", "far17"]
    return gather_final(
        sums,
        first,
        [exps[name] for name in names],
        [blocks[name] for name in names],
        far_trio,
        near_trio,
    )


def solution(mesh):
    placed = (P(("row", "col"), None), P(("row", "col")))
    return jax.shard_map(
        on_device, mesh=mesh, in_specs=placed, out_specs=P(("row", "col"), None), check_vma=False
    )
```

```python
import functools

import jax
import jax.numpy as jnp
from jax import lax
from jax.experimental import pallas as pl
from jax.experimental.pallas import tpu as pltpu
from jax.sharding import PartitionSpec as P

inverse_temp = 5.0
epsilon = 1e-06
both = ("row", "col")
lanes = 128
chunk = 256


def routes(rows, cols):
    count = rows * cols
    far_step = cols
    x_step = count // 4
    line = cols // 2

    def wrap(value):
        return value % count

    def core(b):
        return (b // cols) % 2

    def half(b):
        return (b // (2 * cols)) % 2

    def far17(b):
        j = b % cols
        if core(b) == 0:
            if j == 0:
                return wrap(b + (2 * cols if half(b) == 0 else -2 * cols) + cols - 1)
            return wrap(b - 2 * cols - 1) if j == cols // 2 else b - 1
        if j == cols - 1:
            return wrap(b + (2 * cols if half(b) == 0 else -2 * cols) - cols + 1)
        return wrap(b + 2 * cols + 1) if j == cols // 2 - 1 else b + 1

    def near(b):
        return b + far_step if core(b) == 0 else b - far_step

    def ring(step):
        return lambda b: b - b % line + (b + step) % line

    def turn(b):
        return wrap(b + 1) if (b + 1) % line == 0 else wrap(b - 1) if b % line == 0 else b

    def turn_source(b):
        taken = turn(b)
        if taken == b:
            return near(b)
        return taken + line - 1 if taken % line == 0 else taken - line + 1

    sources = {
        "even": lambda b: b ^ 1,
        "odd": lambda b: wrap(b - 1 if b % 2 == 0 else b + 1),
        "ring_above": ring(1),
        "ring_below": ring(-1),
        "turn": turn_source,
        "x_even": lambda b: wrap(b + x_step if (b // x_step) % 2 == 0 else b - x_step),
        "x_odd": lambda b: wrap(b - x_step if (b // x_step) % 2 == 0 else b + x_step),
        "x_first": lambda b: wrap(b - x_step if core(b) == 0 else b + x_step),
        "x_second": lambda b: wrap(b + x_step if core(b) == 0 else b - x_step),
        "near": near,
        "far": lambda b: wrap(b - far_step if core(b) == 0 else b + far_step),
        "far17": far17,
    }
    corners = [b for b in range(count) if b % cols == (0, cols - 1)[core(b)] and half(b) == core(b)]
    pairs = {name: [(source(b), b) for b in range(count)] for name, source in sources.items()}
    crossing = {s: b for s, b in pairs["far17"] if b in corners}
    idle = {b: near(b) for b in corners}
    idle.update({b: near(b) for b in range(count) if b not in crossing and b not in corners})
    idle.update(crossing)
    pairs["corner"] = sorted(idle.items())
    pairs["row"] = [(b + cols - 1 if b % cols == 0 else b - cols + 1, b) for b in corners]
    free = {s: near(s) for s, b in pairs["far17"] if b in corners}
    pairs["far17"] = [(s, free.get(s, b)) for s, b in pairs["far17"]]
    free = {s: s + line - 1 if s % line == 0 else s - line + 1 for s, b in pairs["turn"] if b in corners}
    pairs["turn"] = [(s, free.get(s, b)) for s, b in pairs["turn"]]
    return pairs


vmem_limit = 5 * 1024 * 1024
held = pl.BlockSpec(memory_space=pltpu.VMEM)
small = pl.BlockSpec(memory_space=pltpu.VMEM)
anywhere = pl.BlockSpec(memory_space=pl.ANY)


def hold(*arrays):
    return [pltpu.with_memory_space_constraint(array, pltpu.VMEM) for array in arrays]


def call(kernel, name, in_specs, out_specs, out_shape, flops, moved, exps=0, scratch=(), aliases={}):
    return pl.pallas_call(
        kernel,
        in_specs=in_specs,
        out_specs=out_specs,
        out_shape=out_shape,
        scratch_shapes=scratch,
        input_output_aliases=aliases,
        compiler_params=pltpu.CompilerParams(vmem_limit_bytes=vmem_limit),
        cost_estimate=pl.CostEstimate(flops=flops, bytes_accessed=moved, transcendentals=exps),
        name=name,
    )


def parts(rows):
    return [slice(start, start + chunk) for start in range(0, rows, chunk)]


def halves(rows):
    return [slice(0, rows // 2), slice(rows // 2, rows)]


def normalize_kernel(rows_ref, out_ref, held_ref, sems):
    rows = rows_ref.shape[0]
    copies = []
    for number, part in enumerate(halves(rows)):
        copy = pltpu.make_async_copy(rows_ref.at[part], held_ref.at[part], sems.at[number])
        copy.start()
        copies.append(copy)
    for copy, part in zip(copies, halves(rows)):
        copy.wait()
        wide = held_ref[part, :].astype(jnp.float32)
        scale = lax.rsqrt(jnp.sum(wide * wide, axis=-1, keepdims=True) + epsilon)
        out_ref[part, :] = (wide * scale).astype(jnp.bfloat16)


def normalize(embeddings):
    rows, width = embeddings.shape
    return call(
        normalize_kernel,
        "normalize",
        [anywhere],
        held,
        pltpu.VMEM((rows, width), jnp.bfloat16),
        4 * rows * width,
        4 * rows * width,
        scratch=[
            pltpu.VMEM((rows, width), jnp.bfloat16),
            pltpu.SemaphoreType.DMA((2,)),
        ],
    )(pltpu.with_memory_space_constraint(embeddings, pltpu.HBM))


def exps_of(mine, theirs):
    scores = lax.dot_general(
        mine, theirs, (((1,), (1,)), ((), ())), preferred_element_type=jnp.float32
    )
    return jnp.exp(scores * inverse_temp)


def fold(exps):
    total = exps[:, :lanes]
    for start in range(lanes, exps.shape[1], lanes):
        total = total + exps[:, start : start + lanes]
    return total


def self_kernel(mine_ref, pos_ref, exps_ref, sums_ref, matched_ref):
    rows = mine_ref.shape[0]
    pairs = [pos_ref[number : number + 1, :] for number in range(rows // lanes)]
    partners = jnp.concatenate(pairs, axis=1)
    for part in parts(rows):
        k = lax.broadcasted_iota(jnp.int32, (chunk, rows), 0) + part.start
        j = lax.broadcasted_iota(jnp.int32, (chunk, rows), 1)
        exps = jnp.where(k == j, 0.0, exps_of(mine_ref[part, :], mine_ref[...]))
        exps_ref[part, :] = exps.astype(jnp.bfloat16)
        sums_ref[part, :] = fold(exps)
        picks = jnp.where(k == partners, 1.0, 0.0).astype(jnp.bfloat16)
        matched = jnp.dot(picks, mine_ref[...], preferred_element_type=jnp.float32)
        matched_ref[part, :] = matched.astype(jnp.bfloat16)


def self_tile(normed, positives):
    rows, width = normed.shape
    return call(
        self_kernel,
        "self_tile",
        [held, small],
        [held] * 3,
        [
            pltpu.VMEM((rows, rows), jnp.bfloat16),
            pltpu.VMEM((rows, lanes), jnp.float32),
            pltpu.VMEM((rows, width), jnp.bfloat16),
        ],
        4 * rows * rows * width,
        4 * rows * width + 2 * rows * rows,
        rows * rows,
    )(*hold(normed), positives)


def tile_kernel(mine_ref, theirs_ref, before_ref, exps_ref, sums_ref):
    for part in parts(mine_ref.shape[0]):
        exps = exps_of(mine_ref[part, :], theirs_ref[...])
        exps_ref[part, :] = exps.astype(jnp.bfloat16)
        sums_ref[part, :] = before_ref[part, :] + fold(exps)


def pair_tile(normed, block, sums):
    rows, width = normed.shape
    return call(
        tile_kernel,
        "pair_tile",
        [held] * 3,
        [held] * 2,
        [pltpu.VMEM((rows, rows), jnp.bfloat16), pltpu.VMEM((rows, lanes), jnp.float32)],
        2 * rows * rows * width,
        4 * rows * width + 2 * rows * rows,
        rows * rows,
    )(*hold(normed, block, sums))


def last_kernel(mine_ref, theirs_ref, before_ref, exps_ref, sums_ref, denoms_ref):
    for part in parts(mine_ref.shape[0]):
        exps = exps_of(mine_ref[part, :], theirs_ref[...])
        exps_ref[part, :] = exps.astype(jnp.bfloat16)
        sums = before_ref[part, :] + fold(exps)
        sums_ref[part, :] = sums
        denoms_ref[:, part] = jnp.sum(sums.T, axis=0, keepdims=True)


def last_tile(normed, block, sums):
    rows, width = normed.shape
    return call(
        last_kernel,
        "last_tile",
        [held] * 3,
        [held] * 3,
        [
            pltpu.VMEM((rows, rows), jnp.bfloat16),
            pltpu.VMEM((rows, lanes), jnp.float32),
            pltpu.VMEM((1, rows), jnp.float32),
        ],
        2 * rows * rows * width,
        4 * rows * width + 2 * rows * rows,
        rows * rows,
    )(*hold(normed, block, sums))


def far17_kernel(far_ref, near_ref, mine_ref, out_ref):
    cols, col = lax.axis_size("col"), lax.axis_index("col")
    core0 = lax.axis_index("row") % 2 == 0
    last = col == jnp.where(core0, cols - 1, 0)
    turn = col == jnp.where(core0, cols // 2 - 1, cols // 2)
    for chosen, ref in [(last, mine_ref), (turn, near_ref), (~last & ~turn, far_ref)]:

        @pl.when(chosen)
        def _():
            out_ref[...] = ref[...]


def at_corner():
    cols, row = lax.axis_size("col"), lax.axis_index("row")
    core, half = row % 2, (row // 2) % 2
    return (lax.axis_index("col") == core * (cols - 1)) & (half == core)


def corner_kernel(far17_ref, corner_ref, out_ref):
    del far17_ref

    @pl.when(at_corner())
    def _():
        out_ref[...] = corner_ref[...]


def turn_kernel(below_ref, above_ref, out_ref):
    line = lax.axis_size("col") // 2
    place = lax.axis_index("col") % line

    @pl.when(place == line - 1)
    def _():
        out_ref[...] = above_ref[...]

    @pl.when(place == 0)
    def _():
        out_ref[...] = below_ref[...]


def merge_kernel(shift, core, ring_ref, turn_ref, row_ref, out_ref):
    turns = (lax.axis_index("col") + shift) % (lax.axis_size("col") // 2) == 0
    corner = at_corner() & (lax.axis_index("row") % 2 == core)
    for chosen, ref in [(~turns, ring_ref), (turns & ~corner, turn_ref), (corner, row_ref)]:

        @pl.when(chosen)
        def _():
            out_ref[...] = ref[...]


def near17_kernel(below_ref, above_ref, out_ref):
    core0 = lax.axis_index("row") % 2 == 0

    @pl.when(core0)
    def _():
        out_ref[...] = below_ref[...]

    @pl.when(~core0)
    def _():
        out_ref[...] = above_ref[...]


def choose(kernel, name, *choices, aliases={}):
    shape = choices[0].shape
    return call(
        kernel,
        name,
        [held] * len(choices),
        held,
        pltpu.VMEM(shape, jnp.bfloat16),
        0,
        4 * shape[0] * shape[1],
        aliases=aliases,
    )(*hold(*choices))


def weighted(sums_ref, others, exps_refs, block_refs, part):
    mine = 1.0 / jnp.sum(sums_ref[part, :], axis=1, keepdims=True)
    total = None
    for other, exps_ref, block_ref in zip(others, exps_refs, block_refs):
        weights = exps_ref[part, :].astype(jnp.float32) * (mine + other)
        term = jnp.dot(
            weights.astype(jnp.bfloat16), block_ref[...], preferred_element_type=jnp.float32
        )
        total = term if total is None else total + term
    return total


def first_kernel(count, sums_ref, matched_ref, *refs):
    exps_refs, block_refs = refs[:count], refs[count : 2 * count]
    trio_ref, x_even_ref, x_odd_ref, out_ref = refs[2 * count :]
    row = lax.axis_index("row")
    even = (row // (lax.axis_size("row") // 4)) % 2 == row % 2
    x_first = jnp.where(even, x_odd_ref[...], x_even_ref[...])
    x_second = jnp.where(even, x_even_ref[...], x_odd_ref[...])
    norms = [trio_ref[0:1, :], trio_ref[1:2, :], trio_ref[2:3, :], x_first, x_second]
    others = [1.0 / norm for norm in norms]
    for part in parts(sums_ref.shape[0]):
        total = weighted(sums_ref, others, exps_refs, block_refs, part)
        out_ref[part, :] = total - 2.0 * matched_ref[part, :].astype(jnp.float32)


def final_kernel(count, sums_ref, first_ref, *refs):
    exps_refs, block_refs = refs[:count], refs[count : 2 * count]
    far_ref, near_ref, out_ref, held_ref, sems = refs[2 * count :]
    core0 = lax.axis_index("row") % 2 == 0
    near17 = jnp.where(core0, near_ref[1:2, :], near_ref[2:3, :])
    far17 = jnp.where(core0, far_ref[2:3, :], far_ref[1:2, :])
    others = [1.0 / norm for norm in (near_ref[0:1, :], far_ref[0:1, :], near17, far17)]
    copies = []
    *most, last = parts(sums_ref.shape[0])
    half = (last.start + last.stop) // 2
    for number, part in enumerate([*most, slice(last.start, half), slice(half, last.stop)]):
        total = weighted(sums_ref, others, exps_refs, block_refs, part)
        held_ref[part, :] = inverse_temp * (first_ref[part, :] + total)
        copy = pltpu.make_async_copy(held_ref.at[part], out_ref.at[part], sems.at[number])
        copy.start()
        copies.append(copy)
    for copy in copies:
        copy.wait()


def gather_first(sums, matched, exps, blocks, norms):
    count, (rows, width) = len(exps), matched.shape
    return call(
        functools.partial(first_kernel, count),
        "gather_first",
        [held] * (2 * count + 5),
        held,
        pltpu.VMEM((rows, width), jnp.float32),
        2 * count * rows * rows * width,
        count * 2 * rows * (rows + width) + 8 * rows * width,
    )(*hold(sums, matched, *exps, *blocks, *norms))


def gather_final(sums, first, exps, blocks, far_trio, near_trio):
    count, (rows, width) = len(exps), first.shape
    return call(
        functools.partial(final_kernel, count),
        "gather_final",
        [held] * (2 * count + 4),
        anywhere,
        jax.ShapeDtypeStruct((rows, width), jnp.float32),
        2 * count * rows * rows * width,
        count * 2 * rows * (rows + width) + 8 * rows * width,
        scratch=[
            pltpu.VMEM((rows, width), jnp.float32),
            pltpu.SemaphoreType.DMA((rows // chunk + 1,)),
        ],
    )(*hold(sums, first, *exps, *blocks, far_trio, near_trio))


def trio_kernel(mine_ref, even_ref, odd_ref, out_ref):
    even = lax.axis_index("col") % 2 == 0
    out_ref[0:1, :] = mine_ref[...]
    out_ref[1:2, :] = jnp.where(even, even_ref[...], odd_ref[...])
    out_ref[2:3, :] = jnp.where(even, odd_ref[...], even_ref[...])


def trio_of(mine, even, odd):
    width = mine.shape[1]
    return call(
        trio_kernel,
        "trio",
        [held] * 3,
        held,
        pltpu.VMEM((3, width), jnp.float32),
        0,
        24 * width,
    )(*hold(mine, even, odd))


def on_device(embeddings, positives):
    rows, cols = lax.axis_size("row"), lax.axis_size("col")
    route = routes(rows, cols)

    def send(block, name):
        return lax.ppermute(block, both, route[name])

    normed = normalize(embeddings)
    near = send(normed, "near")
    ring_below = send(normed, "ring_below")
    ring_above = send(normed, "ring_above")
    far = send(normed, "far")
    self_exps, sums, matched = self_tile(normed, positives.reshape(-1, lanes))
    later, near, sums = lax.optimization_barrier((normed, near, sums))
    x_first = send(later, "x_first")
    x_second = send(later, "x_second")
    ring_below, sums = lax.optimization_barrier((ring_below, sums))
    turn = send(choose(turn_kernel, "turn", ring_below, ring_above), "turn")
    passed = choose(far17_kernel, "far17", far, near, normed)
    far17 = send(passed, "far17")
    far, passed = lax.optimization_barrier((far, passed))
    across = send(far, "row")
    corner = send(x_first, "corner")
    exps, blocks = {}, {}

    def add(sums, **some):
        for name, block in some.items():
            blocks[name] = block
            exps[name], sums = pair_tile(normed, block, sums)
        return sums

    sums = add(sums, near=near, far=far, x_first=x_first, x_second=x_second)
    turn, sums = lax.optimization_barrier((turn, sums))
    above = choose(functools.partial(merge_kernel, 1, 1), "above", ring_above, turn, across)
    below = choose(functools.partial(merge_kernel, 0, 0), "below", ring_below, turn, across)
    near17 = send(choose(near17_kernel, "near17", below, above), "near")
    sums = add(sums, above=above, below=below)
    sums = add(sums, far17=choose(corner_kernel, "corner", far17, corner, aliases={0: 0}))
    blocks["near17"] = near17
    exps["near17"], sums, denoms = last_tile(normed, near17, sums)

    trio = trio_of(denoms, send(denoms, "even"), send(denoms, "odd"))
    d_x_even = send(denoms, "x_even")
    d_x_odd = send(denoms, "x_odd")
    far_trio = send(trio, "far")
    near_trio = send(trio, "near")

    names = ["above", "below", "x_first", "x_second"]
    first = gather_first(
        sums,
        matched,
        [self_exps] + [exps[name] for name in names],
        [normed] + [blocks[name] for name in names],
        [trio, d_x_even, d_x_odd],
    )
    names = ["near", "far", "near17", "far17"]
    return gather_final(
        sums,
        first,
        [exps[name] for name in names],
        [blocks[name] for name in names],
        far_trio,
        near_trio,
    )


def solution(mesh):
    placed = (P(("row", "col"), None), P(("row", "col")))
    return jax.shard_map(
        on_device, mesh=mesh, in_specs=placed, out_specs=P(("row", "col"), None), check_vma=False
    )
```

```python
import functools

import jax
import jax.numpy as jnp
from jax import lax
from jax.experimental import pallas as pl
from jax.experimental.pallas import tpu as pltpu
from jax.sharding import PartitionSpec as P

inverse_temp = 5.0
epsilon = 1e-06
both = ("row", "col")
lanes = 128
chunk = 256


def routes(rows, cols):
    count = rows * cols
    far_step = cols
    x_step = count // 4
    line = cols // 2

    def wrap(value):
        return value % count

    def core(b):
        return (b // cols) % 2

    def half(b):
        return (b // (2 * cols)) % 2

    def far17(b):
        j = b % cols
        if core(b) == 0:
            if j == 0:
                return wrap(b + (2 * cols if half(b) == 0 else -2 * cols) + cols - 1)
            return wrap(b - 2 * cols - 1) if j == cols // 2 else b - 1
        if j == cols - 1:
            return wrap(b + (2 * cols if half(b) == 0 else -2 * cols) - cols + 1)
        return wrap(b + 2 * cols + 1) if j == cols // 2 - 1 else b + 1

    def near(b):
        return b + far_step if core(b) == 0 else b - far_step

    def ring(step):
        return lambda b: b - b % line + (b + step) % line

    def turn(b):
        return wrap(b + 1) if (b + 1) % line == 0 else wrap(b - 1) if b % line == 0 else b

    def turn_source(b):
        taken = turn(b)
        if taken == b:
            return near(b)
        return taken + line - 1 if taken % line == 0 else taken - line + 1

    sources = {
        "even": lambda b: b ^ 1,
        "odd": lambda b: wrap(b - 1 if b % 2 == 0 else b + 1),
        "ring_above": ring(1),
        "ring_below": ring(-1),
        "turn": turn_source,
        "x_even": lambda b: wrap(b + x_step if (b // x_step) % 2 == 0 else b - x_step),
        "x_odd": lambda b: wrap(b - x_step if (b // x_step) % 2 == 0 else b + x_step),
        "x_first": lambda b: wrap(b - x_step if core(b) == 0 else b + x_step),
        "x_second": lambda b: wrap(b + x_step if core(b) == 0 else b - x_step),
        "near": near,
        "far": lambda b: wrap(b - far_step if core(b) == 0 else b + far_step),
        "far17": far17,
    }
    corners = [b for b in range(count) if b % cols == (0, cols - 1)[core(b)] and half(b) == core(b)]
    pairs = {name: [(source(b), b) for b in range(count)] for name, source in sources.items()}
    crossing = {s: b for s, b in pairs["far17"] if b in corners}
    idle = {b: near(b) for b in corners}
    idle.update({b: near(b) for b in range(count) if b not in crossing and b not in corners})
    idle.update(crossing)
    pairs["corner"] = sorted(idle.items())
    pairs["row"] = [(b + cols - 1 if b % cols == 0 else b - cols + 1, b) for b in corners]
    free = {s: near(s) for s, b in pairs["far17"] if b in corners}
    pairs["far17"] = [(s, free.get(s, b)) for s, b in pairs["far17"]]
    free = {s: s + line - 1 if s % line == 0 else s - line + 1 for s, b in pairs["turn"] if b in corners}
    pairs["turn"] = [(s, free.get(s, b)) for s, b in pairs["turn"]]
    return pairs


vmem_limit = 5 * 1024 * 1024
held = pl.BlockSpec(memory_space=pltpu.VMEM)
small = pl.BlockSpec(memory_space=pltpu.VMEM)
anywhere = pl.BlockSpec(memory_space=pl.ANY)


def hold(*arrays):
    return [pltpu.with_memory_space_constraint(array, pltpu.VMEM) for array in arrays]


def call(kernel, name, in_specs, out_specs, out_shape, flops, moved, exps=0, scratch=(), aliases={}):
    return pl.pallas_call(
        kernel,
        in_specs=in_specs,
        out_specs=out_specs,
        out_shape=out_shape,
        scratch_shapes=scratch,
        input_output_aliases=aliases,
        compiler_params=pltpu.CompilerParams(vmem_limit_bytes=vmem_limit),
        cost_estimate=pl.CostEstimate(flops=flops, bytes_accessed=moved, transcendentals=exps),
        name=name,
    )


def parts(rows):
    return [slice(start, start + chunk) for start in range(0, rows, chunk)]


def halves(rows):
    return [slice(0, rows // 2), slice(rows // 2, rows)]


def normalize_kernel(rows_ref, out_ref, held_ref, sems):
    rows = rows_ref.shape[0]
    copies = []
    for number, part in enumerate(halves(rows)):
        copy = pltpu.make_async_copy(rows_ref.at[part], held_ref.at[part], sems.at[number])
        copy.start()
        copies.append(copy)
    for copy, part in zip(copies, halves(rows)):
        copy.wait()
        wide = held_ref[part, :].astype(jnp.float32)
        scale = lax.rsqrt(jnp.sum(wide * wide, axis=-1, keepdims=True) + epsilon)
        out_ref[part, :] = (wide * scale).astype(jnp.bfloat16)


def normalize(embeddings):
    rows, width = embeddings.shape
    return call(
        normalize_kernel,
        "normalize",
        [anywhere],
        held,
        pltpu.VMEM((rows, width), jnp.bfloat16),
        4 * rows * width,
        4 * rows * width,
        scratch=[
            pltpu.VMEM((rows, width), jnp.bfloat16),
            pltpu.SemaphoreType.DMA((2,)),
        ],
    )(pltpu.with_memory_space_constraint(embeddings, pltpu.HBM))


def exps_of(mine, theirs):
    scores = lax.dot_general(
        mine, theirs, (((1,), (1,)), ((), ())), preferred_element_type=jnp.float32
    )
    return jnp.exp(scores * inverse_temp)


def fold(exps):
    total = exps[:, :lanes]
    for start in range(lanes, exps.shape[1], lanes):
        total = total + exps[:, start : start + lanes]
    return total


def self_kernel(mine_ref, pos_ref, exps_ref, sums_ref, matched_ref):
    rows = mine_ref.shape[0]
    pairs = [pos_ref[number : number + 1, :] for number in range(rows // lanes)]
    partners = jnp.concatenate(pairs, axis=1)
    for part in parts(rows):
        k = lax.broadcasted_iota(jnp.int32, (chunk, rows), 0) + part.start
        j = lax.broadcasted_iota(jnp.int32, (chunk, rows), 1)
        exps = jnp.where(k == j, 0.0, exps_of(mine_ref[part, :], mine_ref[...]))
        exps_ref[part, :] = exps.astype(jnp.bfloat16)
        sums_ref[part, :] = fold(exps)
        picks = jnp.where(k == partners, 1.0, 0.0).astype(jnp.bfloat16)
        matched = jnp.dot(picks, mine_ref[...], preferred_element_type=jnp.float32)
        matched_ref[part, :] = matched.astype(jnp.bfloat16)


def self_tile(normed, positives):
    rows, width = normed.shape
    return call(
        self_kernel,
        "self_tile",
        [held, small],
        [held] * 3,
        [
            pltpu.VMEM((rows, rows), jnp.bfloat16),
            pltpu.VMEM((rows, lanes), jnp.float32),
            pltpu.VMEM((rows, width), jnp.bfloat16),
        ],
        4 * rows * rows * width,
        4 * rows * width + 2 * rows * rows,
        rows * rows,
    )(*hold(normed), positives)


def tile_kernel(mine_ref, theirs_ref, before_ref, exps_ref, sums_ref):
    for part in parts(mine_ref.shape[0]):
        exps = exps_of(mine_ref[part, :], theirs_ref[...])
        exps_ref[part, :] = exps.astype(jnp.bfloat16)
        sums_ref[part, :] = before_ref[part, :] + fold(exps)


def pair_tile(normed, block, sums):
    rows, width = normed.shape
    return call(
        tile_kernel,
        "pair_tile",
        [held] * 3,
        [held] * 2,
        [pltpu.VMEM((rows, rows), jnp.bfloat16), pltpu.VMEM((rows, lanes), jnp.float32)],
        2 * rows * rows * width,
        4 * rows * width + 2 * rows * rows,
        rows * rows,
    )(*hold(normed, block, sums))


def last_kernel(mine_ref, theirs_ref, before_ref, exps_ref, sums_ref, denoms_ref):
    for part in parts(mine_ref.shape[0]):
        exps = exps_of(mine_ref[part, :], theirs_ref[...])
        exps_ref[part, :] = exps.astype(jnp.bfloat16)
        sums = before_ref[part, :] + fold(exps)
        sums_ref[part, :] = sums
        denoms_ref[:, part] = jnp.sum(sums.T, axis=0, keepdims=True)


def last_tile(normed, block, sums):
    rows, width = normed.shape
    return call(
        last_kernel,
        "last_tile",
        [held] * 3,
        [held] * 3,
        [
            pltpu.VMEM((rows, rows), jnp.bfloat16),
            pltpu.VMEM((rows, lanes), jnp.float32),
            pltpu.VMEM((1, rows), jnp.float32),
        ],
        2 * rows * rows * width,
        4 * rows * width + 2 * rows * rows,
        rows * rows,
    )(*hold(normed, block, sums))


def far17_kernel(far_ref, near_ref, mine_ref, out_ref):
    cols, col = lax.axis_size("col"), lax.axis_index("col")
    core0 = lax.axis_index("row") % 2 == 0
    last = col == jnp.where(core0, cols - 1, 0)
    turn = col == jnp.where(core0, cols // 2 - 1, cols // 2)
    for chosen, ref in [(last, mine_ref), (turn, near_ref), (~last & ~turn, far_ref)]:

        @pl.when(chosen)
        def _():
            out_ref[...] = ref[...]


def at_corner():
    cols, row = lax.axis_size("col"), lax.axis_index("row")
    core, half = row % 2, (row // 2) % 2
    return (lax.axis_index("col") == core * (cols - 1)) & (half == core)


def corner_kernel(far17_ref, corner_ref, out_ref):
    del far17_ref

    @pl.when(at_corner())
    def _():
        out_ref[...] = corner_ref[...]


def turn_kernel(below_ref, above_ref, out_ref):
    line = lax.axis_size("col") // 2
    place = lax.axis_index("col") % line

    @pl.when(place == line - 1)
    def _():
        out_ref[...] = above_ref[...]

    @pl.when(place == 0)
    def _():
        out_ref[...] = below_ref[...]


def merge_kernel(shift, core, ring_ref, turn_ref, row_ref, out_ref):
    turns = (lax.axis_index("col") + shift) % (lax.axis_size("col") // 2) == 0
    corner = at_corner() & (lax.axis_index("row") % 2 == core)
    for chosen, ref in [(~turns, ring_ref), (turns & ~corner, turn_ref), (corner, row_ref)]:

        @pl.when(chosen)
        def _():
            out_ref[...] = ref[...]


def near17_kernel(below_ref, above_ref, turn_ref, row_ref, out_ref):
    line, col = lax.axis_size("col") // 2, lax.axis_index("col")
    core0 = lax.axis_index("row") % 2 == 0
    turns = jnp.where(core0, col, col + 1) % line == 0
    corner = at_corner()
    choices = [
        (~turns & core0, below_ref),
        (~turns & ~core0, above_ref),
        (turns & ~corner, turn_ref),
        (corner, row_ref),
    ]
    for chosen, ref in choices:

        @pl.when(chosen)
        def _():
            out_ref[...] = ref[...]


def choose(kernel, name, *choices, aliases={}):
    shape = choices[0].shape
    return call(
        kernel,
        name,
        [held] * len(choices),
        held,
        pltpu.VMEM(shape, jnp.bfloat16),
        0,
        4 * shape[0] * shape[1],
        aliases=aliases,
    )(*hold(*choices))


def weighted(sums_ref, others, exps_refs, block_refs, part):
    mine = 1.0 / jnp.sum(sums_ref[part, :], axis=1, keepdims=True)
    total = None
    for other, exps_ref, block_ref in zip(others, exps_refs, block_refs):
        weights = exps_ref[part, :].astype(jnp.float32) * (mine + other)
        term = jnp.dot(
            weights.astype(jnp.bfloat16), block_ref[...], preferred_element_type=jnp.float32
        )
        total = term if total is None else total + term
    return total


def first_kernel(count, sums_ref, matched_ref, *refs):
    exps_refs, block_refs = refs[:count], refs[count : 2 * count]
    trio_ref, x_even_ref, x_odd_ref, out_ref = refs[2 * count :]
    row = lax.axis_index("row")
    even = (row // (lax.axis_size("row") // 4)) % 2 == row % 2
    x_first = jnp.where(even, x_odd_ref[...], x_even_ref[...])
    x_second = jnp.where(even, x_even_ref[...], x_odd_ref[...])
    norms = [trio_ref[0:1, :], trio_ref[1:2, :], trio_ref[2:3, :], x_first, x_second]
    others = [1.0 / norm for norm in norms]
    for part in parts(sums_ref.shape[0]):
        total = weighted(sums_ref, others, exps_refs, block_refs, part)
        out_ref[part, :] = total - 2.0 * matched_ref[part, :].astype(jnp.float32)


def final_kernel(count, sums_ref, first_ref, *refs):
    exps_refs, block_refs = refs[:count], refs[count : 2 * count]
    far_ref, near_ref, out_ref, held_ref, sems = refs[2 * count :]
    core0 = lax.axis_index("row") % 2 == 0
    near17 = jnp.where(core0, near_ref[1:2, :], near_ref[2:3, :])
    far17 = jnp.where(core0, far_ref[2:3, :], far_ref[1:2, :])
    others = [1.0 / norm for norm in (near_ref[0:1, :], far_ref[0:1, :], near17, far17)]
    copies = []
    *most, last = parts(sums_ref.shape[0])
    half = (last.start + last.stop) // 2
    for number, part in enumerate([*most, slice(last.start, half), slice(half, last.stop)]):
        total = weighted(sums_ref, others, exps_refs, block_refs, part)
        held_ref[part, :] = inverse_temp * (first_ref[part, :] + total)
        copy = pltpu.make_async_copy(held_ref.at[part], out_ref.at[part], sems.at[number])
        copy.start()
        copies.append(copy)
    for copy in copies:
        copy.wait()


def gather_first(sums, matched, exps, blocks, norms):
    count, (rows, width) = len(exps), matched.shape
    return call(
        functools.partial(first_kernel, count),
        "gather_first",
        [held] * (2 * count + 5),
        held,
        pltpu.VMEM((rows, width), jnp.float32),
        2 * count * rows * rows * width,
        count * 2 * rows * (rows + width) + 8 * rows * width,
    )(*hold(sums, matched, *exps, *blocks, *norms))


def gather_final(sums, first, exps, blocks, far_trio, near_trio):
    count, (rows, width) = len(exps), first.shape
    return call(
        functools.partial(final_kernel, count),
        "gather_final",
        [held] * (2 * count + 4),
        anywhere,
        jax.ShapeDtypeStruct((rows, width), jnp.float32),
        2 * count * rows * rows * width,
        count * 2 * rows * (rows + width) + 8 * rows * width,
        scratch=[
            pltpu.VMEM((rows, width), jnp.float32),
            pltpu.SemaphoreType.DMA((rows // chunk + 1,)),
        ],
    )(*hold(sums, first, *exps, *blocks, far_trio, near_trio))


def trio_kernel(mine_ref, even_ref, odd_ref, out_ref):
    even = lax.axis_index("col") % 2 == 0
    out_ref[0:1, :] = mine_ref[...]
    out_ref[1:2, :] = jnp.where(even, even_ref[...], odd_ref[...])
    out_ref[2:3, :] = jnp.where(even, odd_ref[...], even_ref[...])


def trio_of(mine, even, odd):
    width = mine.shape[1]
    return call(
        trio_kernel,
        "trio",
        [held] * 3,
        held,
        pltpu.VMEM((3, width), jnp.float32),
        0,
        24 * width,
    )(*hold(mine, even, odd))


def on_device(embeddings, positives):
    rows, cols = lax.axis_size("row"), lax.axis_size("col")
    route = routes(rows, cols)

    def send(block, name):
        return lax.ppermute(block, both, route[name])

    normed = normalize(embeddings)
    near = send(normed, "near")
    ring_below = send(normed, "ring_below")
    ring_above = send(normed, "ring_above")
    far = send(normed, "far")
    self_exps, sums, matched = self_tile(normed, positives.reshape(-1, lanes))
    later, near, sums = lax.optimization_barrier((normed, near, sums))
    x_first = send(later, "x_first")
    x_second = send(later, "x_second")
    ring_below, sums = lax.optimization_barrier((ring_below, sums))
    turn = send(choose(turn_kernel, "turn", ring_below, ring_above), "turn")
    passed = choose(far17_kernel, "far17", far, near, normed)
    far17 = send(passed, "far17")
    far, passed = lax.optimization_barrier((far, passed))
    across = send(far, "row")
    corner = send(x_first, "corner")
    exps, blocks = {}, {}

    def add(sums, **some):
        for name, block in some.items():
            blocks[name] = block
            exps[name], sums = pair_tile(normed, block, sums)
        return sums

    sums = add(sums, near=near, far=far, x_first=x_first, x_second=x_second)
    turn, sums = lax.optimization_barrier((turn, sums))
    near17 = send(
        choose(near17_kernel, "near17", ring_below, ring_above, turn, across), "near"
    )
    above = choose(functools.partial(merge_kernel, 1, 1), "above", ring_above, turn, across)
    below = choose(functools.partial(merge_kernel, 0, 0), "below", ring_below, turn, across)
    sums = add(sums, above=above, below=below)
    sums = add(sums, far17=choose(corner_kernel, "corner", far17, corner, aliases={0: 0}))
    blocks["near17"] = near17
    exps["near17"], sums, denoms = last_tile(normed, near17, sums)

    trio = trio_of(denoms, send(denoms, "even"), send(denoms, "odd"))
    d_x_even = send(denoms, "x_even")
    d_x_odd = send(denoms, "x_odd")
    far_trio = send(trio, "far")
    near_trio = send(trio, "near")

    names = ["above", "below", "x_first", "x_second"]
    first = gather_first(
        sums,
        matched,
        [self_exps] + [exps[name] for name in names],
        [normed] + [blocks[name] for name in names],
        [trio, d_x_even, d_x_odd],
    )
    names = ["near", "far", "near17", "far17"]
    return gather_final(
        sums,
        first,
        [exps[name] for name in names],
        [blocks[name] for name in names],
        far_trio,
        near_trio,
    )


def solution(mesh):
    placed = (P(("row", "col"), None), P(("row", "col")))
    return jax.shard_map(
        on_device, mesh=mesh, in_specs=placed, out_specs=P(("row", "col"), None), check_vma=False
    )
```
